32 devices in a mesh: grp: 4 (over y, x), wide: 8 (over z, core).
Axes of the slice: x: 2, y: 2, z: 4, core: 2. Of those that a mesh axis runs over, the one named last changes fastest.
Arguments:
- embeddings: float32 [49152, 768], P(('grp', 'wide')), may hold values from -200 to 200, as said below
Outputs:
- whitened: float32 [49152, 768], P(('grp', 'wide'))
- factor_scaled: float32 [768, 768], replicated
The draws below stay inside these ranges and needn't reach their ends.
Inputs may be any that keep to these rules, and one draw needn't show every extreme that they name: `embeddings`: Real-valued rows; no structure is promised.
All inputs are finite; a program needn't handle non-finite values.
Results may differ from the reference program's by a relative error of at most 0.000054.
Values sent between devices are 32-bit elements; how exact they have to be, the bound alone decides.
No kernel may reach another device: no remote copies, remote signals or barrier semaphores. Data moves between devices by JAX's collectives and lax.ppermute only.
A program may use at most 128 MiB of HBM per device.

```python
import math
import jax
import jax.numpy as jnp
from jax import lax

W = 768
ROWS = 49152


def draw_embeddings(key, part):
    key = jax.random.fold_in(key, 1)
    key_scale, key_offset, key_noise = jax.random.split(key, 3)
    top = math.log(10.0)
    noise = jnp.clip(jax.random.normal(key_noise, (ROWS, W), jnp.float32), -6.0, 6.0)
    col_scale = jnp.exp(jax.random.uniform(key_scale, (W,), jnp.float32, 0.0, top))
    offsets = jax.random.uniform(key_offset, (W,), jnp.float32, -3.0, 3.0)
    position = jnp.arange(ROWS, dtype=jnp.float32) / ROWS
    row_scale = 1.0 + 2.0 * position
    return offsets[None, :] + row_scale[:, None] * col_scale[None, :] * noise


def setup_inputs(seed: int = 0) -> dict:
    key_of = jax.random.split(jax.random.key(seed), 2)
    embeddings = draw_embeddings(jax.random.fold_in(key_of[1], 71), 0)
    return {"embeddings": embeddings}


def reference(embeddings):
    row_count = embeddings.shape[0]
    col_mean = lax.optimization_barrier(jnp.sum(embeddings, axis=0)) / row_count
    centred = embeddings - col_mean[None, :]
    gram = lax.dot_general(centred.astype(jnp.float32), centred.astype(jnp.float32), (((0,), (0,)), ((), ())), precision=lax.Precision.HIGHEST, preferred_element_type=jnp.float32)
    lower = jnp.linalg.cholesky(gram)
    factor = lower.T
    scale = jnp.sqrt(jnp.float32(row_count))
    solved = jax.scipy.linalg.solve_triangular(lower, centred.T, lower=True)
    whitened = solved.T * scale
    return (whitened, factor / scale)
```

```python
import jax
import jax.numpy as jnp
from jax import lax
from jax.experimental import pallas as pl
from jax.experimental.pallas import tpu as pltpu
from jax.sharding import PartitionSpec as P

AXES = ("grp", "wide")
LANES = 128
SUB = 8
HIGHEST = lax.Precision.HIGHEST


def dot(a, b, dims):
    return lax.dot_general(
        a, b, (dims, ((), ())), precision=HIGHEST, preferred_element_type=jnp.float32
    )


def over_lanes(tile, lane):
    return jnp.broadcast_to(tile[:, lane : lane + 1], (SUB, LANES))


def over_rows(tile, row):
    return jnp.broadcast_to(tile[row : row + 1, :], (SUB, LANES))


def factor_block(block, upper_ref, inverse_ref):
    groups = LANES // SUB
    tiles = [block[SUB * p : SUB * (p + 1), :] for p in range(groups)]
    row_at = lax.broadcasted_iota(jnp.int32, (SUB, LANES), 0)
    lane_at = lax.broadcasted_iota(jnp.int32, (SUB, LANES), 1)
    unit = [
        jnp.where(lane_at == row_at + SUB * p, 1.0, 0.0).astype(jnp.float32)
        for p in range(groups)
    ]
    for g in range(groups):
        base = SUB * g
        rows = [over_rows(tiles[g], i) for i in range(SUB)]
        carried = [over_rows(unit[g], i) for i in range(SUB)]
        s = {
            (i, j): over_lanes(rows[i], base + j) for i in range(SUB) for j in range(i, SUB)
        }
        scale = []
        for j in range(SUB):
            r = lax.rsqrt(s[j, j])
            scale.append(r)
            rows[j] = rows[j] * r
            carried[j] = carried[j] * r
            for k in range(j + 1, SUB):
                s[j, k] = s[j, k] * r
            for k in range(j + 1, SUB):
                for m in range(k, SUB):
                    s[k, m] = s[k, m] - s[j, k] * s[j, m]
                rows[k] = rows[k] - s[j, k] * rows[j]
                carried[k] = carried[k] - s[j, k] * carried[j]
            upper_ref[base + j : base + j + 1, :] = rows[j][:1, :]
            inverse_ref[base + j : base + j + 1, :] = carried[j][:1, :]
        if g == groups - 1:
            break
        for i in reversed(range(SUB)):
            for k in range(i + 1, SUB):
                rows[i] = rows[i] - s[i, k] * rows[k]
                carried[i] = carried[i] - s[i, k] * carried[k]
            rows[i] = rows[i] * scale[i]
            carried[i] = carried[i] * scale[i]
        for p in range(g + 1, groups):
            column = [over_lanes(tiles[p], base + i) for i in range(SUB)]
            tiles[p] = tiles[p] - sum(c * x for c, x in zip(column, rows))
            unit[p] = unit[p] - sum(c * x for c, x in zip(column, carried))


def factor_kernel(gram_ref, means_ref, count_ref, factor_ref, inverse_ref, work, upper, inverse):
    width = gram_ref.shape[0]
    blocks = width // LANES
    means = means_ref[...]
    apart = means - jnp.mean(means, axis=0, keepdims=True)
    between = dot(apart, apart, ((0,), (0,)))
    work[...] = gram_ref[...] + between * count_ref[0]
    total_scale = count_ref[1]
    row_at = lax.broadcasted_iota(jnp.int32, (LANES, width), 0)
    col_at = lax.broadcasted_iota(jnp.int32, (LANES, width), 1)

    def stage(k, _):
        start = pl.multiple_of(k * LANES, LANES)
        here = pl.ds(start, LANES)
        factor_block(work[here, here], upper, inverse)
        solved = dot(inverse[...], work[here, :], ((1,), (0,)))
        work[here, :] = solved
        work[here, here] = upper[...]
        factor_ref[here, :] = jnp.where(
            col_at >= row_at + start, work[here, :] * (1.0 / total_scale), 0.0
        )
        work[here, here] = inverse[...]
        inverse_ref[here, :] = jnp.where(
            col_at <= row_at + start, work[here, :] * total_scale, 0.0
        )

        def below(i, _):
            there = pl.ds(pl.multiple_of(i * LANES, LANES), LANES)
            work[there, here] = jnp.zeros((LANES, LANES), jnp.float32)
            work[there, :] = work[there, :] - dot(
                work[here, there], work[here, :], ((0,), (0,))
            )
            return 0

        lax.fori_loop(k + 1, blocks, below, 0)
        return 0

    lax.fori_loop(0, blocks, stage, 0)


def factor_and_inverse(gram, means, local_rows, row_count):
    width = gram.shape[0]
    square = jax.ShapeDtypeStruct((width, width), jnp.float32)
    counts = jnp.array([local_rows, row_count**0.5], jnp.float32)
    return pl.pallas_call(
        factor_kernel,
        out_shape=(square, square),
        in_specs=[
            pl.BlockSpec(memory_space=pltpu.VMEM),
            pl.BlockSpec(memory_space=pltpu.VMEM),
            pl.BlockSpec(memory_space=pltpu.SMEM),
        ],
        out_specs=(pl.BlockSpec(memory_space=pltpu.VMEM),) * 2,
        scratch_shapes=[
            pltpu.VMEM((width, width), jnp.float32),
            pltpu.VMEM((LANES, LANES), jnp.float32),
            pltpu.VMEM((LANES, LANES), jnp.float32),
        ],
        compiler_params=pltpu.CompilerParams(vmem_limit_bytes=40 * 2**20),
    )(gram, means, counts)


def shards(embeddings):
    local_rows, width = embeddings.shape
    devices = lax.axis_size("grp") * lax.axis_size("wide")
    row_count = local_rows * devices
    me = lax.axis_index(AXES)
    mean = jnp.sum(embeddings, axis=0, keepdims=True) / local_rows
    centred = embeddings - mean
    gram = dot(centred, centred, ((0,), (0,)))
    mine = lax.broadcasted_iota(jnp.int32, (devices, 1), 0) == me
    payload = jnp.concatenate([gram, jnp.where(mine, mean, 0.0)], axis=0)
    payload = lax.psum(payload, AXES)
    means = payload[width:]
    factor, inverse = factor_and_inverse(payload[:width], means, local_rows, row_count)
    col_mean = jnp.mean(means, axis=0, keepdims=True)
    whitened = dot(embeddings - col_mean, inverse, ((1,), (1,)))
    return (whitened, factor)


def solution(mesh):
    rows = P(AXES, None)
    return jax.shard_map(
        shards,
        mesh=mesh,
        in_specs=(rows,),
        out_specs=(rows, P()),
        check_vma=False,
    )
```

```python
import jax
import jax.numpy as jnp
from jax import lax
from jax.experimental import pallas as pl
from jax.experimental.pallas import tpu as pltpu
from jax.sharding import PartitionSpec as P

AXES = ("grp", "wide")
LANES = 128
SUB = 8
TILE = 256
HIGHEST = lax.Precision.HIGHEST


def dot(a, b, dims):
    return lax.dot_general(
        a, b, (dims, ((), ())), precision=HIGHEST, preferred_element_type=jnp.float32
    )


def over_lanes(tile, lane):
    return jnp.broadcast_to(tile[:, lane : lane + 1], (SUB, LANES))


def over_rows(tile, row):
    return jnp.broadcast_to(tile[row : row + 1, :], (SUB, LANES))


def factor_block(block, upper_ref, inverse_ref):
    groups = LANES // SUB
    tiles = [block[SUB * p : SUB * (p + 1), :] for p in range(groups)]
    row_at = lax.broadcasted_iota(jnp.int32, (SUB, LANES), 0)
    lane_at = lax.broadcasted_iota(jnp.int32, (SUB, LANES), 1)
    unit = [
        jnp.where(lane_at == row_at + SUB * p, 1.0, 0.0).astype(jnp.float32)
        for p in range(groups)
    ]
    for g in range(groups):
        base = SUB * g
        rows = [over_rows(tiles[g], i) for i in range(SUB)]
        carried = [over_rows(unit[g], i) for i in range(SUB)]
        s = {
            (i, j): over_lanes(rows[i], base + j) for i in range(SUB) for j in range(i, SUB)
        }
        scale = []
        for j in range(SUB):
            r = lax.rsqrt(s[j, j])
            scale.append(r)
            rows[j] = rows[j] * r
            carried[j] = carried[j] * r
            for k in range(j + 1, SUB):
                s[j, k] = s[j, k] * r
            for k in range(j + 1, SUB):
                for m in range(k, SUB):
                    s[k, m] = s[k, m] - s[j, k] * s[j, m]
                rows[k] = rows[k] - s[j, k] * rows[j]
                carried[k] = carried[k] - s[j, k] * carried[j]
            upper_ref[base + j : base + j + 1, :] = rows[j][:1, :]
            inverse_ref[base + j : base + j + 1, :] = carried[j][:1, :]
        if g == groups - 1:
            break
        for i in reversed(range(SUB)):
            for k in range(i + 1, SUB):
                rows[i] = rows[i] - s[i, k] * rows[k]
                carried[i] = carried[i] - s[i, k] * carried[k]
            rows[i] = rows[i] * scale[i]
            carried[i] = carried[i] * scale[i]
        for p in range(g + 1, groups):
            column = [over_lanes(tiles[p], base + i) for i in range(SUB)]
            tiles[p] = tiles[p] - sum(c * x for c, x in zip(column, rows))
            unit[p] = unit[p] - sum(c * x for c, x in zip(column, carried))


def split(values):
    high = values.astype(jnp.bfloat16)
    return high, (values - high.astype(jnp.float32)).astype(jnp.bfloat16)


def fast_dot(a, b, dims):
    return lax.dot_general(a, b, (dims, ((), ())), preferred_element_type=jnp.float32)


def upper_blocks(width):
    n = width // LANES
    return [(i, j) for i in range(n) for j in range(i, n)]


def gram_kernel(x_ref, packed_ref, mean_ref, both_ref, swapped_ref):
    rows, width = x_ref.shape
    total = jnp.zeros((SUB, width), jnp.float32)
    for r in range(0, rows, LANES):
        part = x_ref[r : r + LANES, :]
        for q in range(0, LANES, SUB):
            total = total + part[q : q + SUB, :]
    mean = jnp.sum(total, axis=0, keepdims=True) * (1.0 / rows)
    for r in range(0, rows, LANES):
        high, low = split(x_ref[r : r + LANES, :] - mean)
        both_ref[r : r + LANES, :] = high
        both_ref[rows + r : rows + r + LANES, :] = low
        swapped_ref[r : r + LANES, :] = low
        swapped_ref[rows + r : rows + r + LANES, :] = high
    place = {block: LANES * p for p, block in enumerate(upper_blocks(width))}
    for left in range(0, width, TILE):
        turned = both_ref[:, left : left + TILE].T
        for right in range(left, width, TILE):
            here = slice(right, right + TILE)
            tile = fast_dot(turned, both_ref[:, here], ((1,), (0,)))
            tile = tile + fast_dot(turned, swapped_ref[:, here], ((1,), (0,)))
            for a in range(0, TILE, LANES):
                for b in range(0, TILE, LANES):
                    block = ((left + a) // LANES, (right + b) // LANES)
                    if block in place:
                        packed_ref[place[block] : place[block] + LANES, :] = tile[
                            a : a + LANES, b : b + LANES
                        ]
    used = LANES * len(place)
    if packed_ref.shape[0] > used:
        packed_ref[used:, :] = jnp.zeros((packed_ref.shape[0] - used, LANES), jnp.float32)
    mean_ref[...] = jnp.zeros(mean_ref.shape, jnp.float32)
    for b in range(width // LANES):
        mean_ref[b : b + 1, :] = mean[:, LANES * b : LANES * (b + 1)]


def local_gram(embeddings, packed_rows, mean_rows):
    rows, width = embeddings.shape
    return pl.pallas_call(
        gram_kernel,
        out_shape=(
            jax.ShapeDtypeStruct((packed_rows, LANES), jnp.float32),
            jax.ShapeDtypeStruct((mean_rows, LANES), jnp.float32),
        ),
        in_specs=[pl.BlockSpec(memory_space=pltpu.VMEM)],
        out_specs=(pl.BlockSpec(memory_space=pltpu.VMEM),) * 2,
        scratch_shapes=[pltpu.VMEM((2 * rows, width), jnp.bfloat16)] * 2,
        compiler_params=pltpu.CompilerParams(vmem_limit_bytes=48 * 2**20),
    )(embeddings)


def exchange_orders(bits):
    body = [b for b in (3, 1) + tuple(range(4, bits)) if b < bits]
    tail = [2] if bits > 2 else []
    return [0] + body + tail, [0] + body[-1:] + body[:-1] + tail


def sum_in_pieces(packed, mean_rows):
    devices = lax.axis_size("grp") * lax.axis_size("wide")
    bits = devices.bit_length() - 1
    orders = exchange_orders(bits)
    me = lax.axis_index(AXES)
    on_core = me & 1

    def partners(step):
        return [(d, d ^ (1 << orders[d & 1][step])) for d in range(devices)]

    def bit_at(step, core):
        return jnp.where(core == 0, me >> orders[0][step], me >> orders[1][step]) & 1

    mine, twin = on_core, 1 - on_core
    for step in range(1, bits):
        mine = mine * 2 + bit_at(step, on_core)
        twin = twin * 2 + bit_at(step, 1 - on_core)
    piece = packed
    for step in range(bits):
        bit = bit_at(step, on_core)
        half = piece.shape[0] // 2
        sent = lax.dynamic_slice_in_dim(piece, (1 - bit) * half, half, 0)
        kept = lax.dynamic_slice_in_dim(piece, bit * half, half, 0)
        piece = kept + lax.ppermute(sent, AXES, partners(step))
    held = jnp.concatenate([piece, mean_rows], axis=0)[None]
    for step in reversed(range(bits)):
        other = lax.ppermute(held, AXES, partners(step))
        if step:
            held = jnp.concatenate([held, other], axis=0)
    return held, other, jnp.stack([mine, twin])


def factor_kernel(
    held_ref,
    other_ref,
    numbers_ref,
    count_ref,
    factor_ref,
    high_ref,
    low_ref,
    mean_ref,
    work,
    packed,
    means_scr,
    upper,
    inverse,
):
    half = held_ref.shape[0]
    pieces = 2 * half
    width = factor_ref.shape[0]
    blocks = width // LANES
    piece_rows = packed.shape[0] // pieces
    for part, ref in enumerate((held_ref, other_ref)):

        def unpack(q, _):
            p = numbers_ref[part] ^ q
            to = pl.multiple_of(p * piece_rows, SUB)
            packed[pl.ds(to, piece_rows), :] = ref[q, :piece_rows, :]
            to = pl.multiple_of(p * SUB, SUB)
            means_scr[pl.ds(to, SUB), :] = ref[q, piece_rows : piece_rows + SUB, :]
            return 0

        lax.fori_loop(0, half, unpack, 0, unroll=True)

    stacked = means_scr[...].reshape(pieces, SUB, LANES)
    middle = jnp.mean(stacked, axis=0)
    apart = stacked - middle[None]
    wide = jnp.concatenate([apart[:, b, :] for b in range(blocks)], axis=1)
    for b in range(blocks):
        mean_ref[:, LANES * b : LANES * (b + 1)] = jnp.broadcast_to(
            middle[b : b + 1, :], (SUB, LANES)
        )
    at = 0
    for i in range(blocks):
        rows = slice(LANES * i, LANES * (i + 1))
        between = dot(wide[:, rows], wide[:, LANES * i :], ((0,), (0,))) * count_ref[0]
        for j in range(i, blocks):
            work[rows, LANES * j : LANES * (j + 1)] = (
                packed[at : at + LANES, :]
                + between[:, LANES * (j - i) : LANES * (j - i + 1)]
            )
            at += LANES
    total_scale = count_ref[1]
    row_at = lax.broadcasted_iota(jnp.int32, (LANES, width), 0)
    col_at = lax.broadcasted_iota(jnp.int32, (LANES, width), 1)

    def stage(k, _):
        start = pl.multiple_of(k * LANES, LANES)
        here = pl.ds(start, LANES)
        factor_block(work[here, here], upper, inverse)
        solved = dot(inverse[...], work[here, :], ((1,), (0,)))
        work[here, :] = solved
        work[here, here] = upper[...]
        factor_ref[here, :] = jnp.where(
            col_at >= row_at + start, work[here, :] * (1.0 / total_scale), 0.0
        )
        work[here, here] = inverse[...]
        high, low = split(
            jnp.where(col_at <= row_at + start, work[here, :] * total_scale, 0.0)
        )
        high_ref[here, :] = high
        low_ref[here, :] = low

        def below(i, _):
            there = pl.ds(pl.multiple_of(i * LANES, LANES), LANES)
            work[there, here] = jnp.zeros((LANES, LANES), jnp.float32)
            work[there, :] = work[there, :] - dot(
                work[here, there], work[here, :], ((0,), (0,))
            )
            return 0

        lax.fori_loop(k + 1, blocks, below, 0)
        return 0

    lax.fori_loop(0, blocks, stage, 0)


def factor_and_inverse(held, other, numbers, piece_rows, width, local_rows):
    pieces = 2 * held.shape[0]
    vmem = pl.BlockSpec(memory_space=pltpu.VMEM)
    smem = pl.BlockSpec(memory_space=pltpu.SMEM)
    half_type = jax.ShapeDtypeStruct((width, width), jnp.bfloat16)
    counts = jnp.array([local_rows, (local_rows * pieces) ** 0.5], jnp.float32)
    return pl.pallas_call(
        factor_kernel,
        out_shape=(
            jax.ShapeDtypeStruct((width, width), jnp.float32),
            half_type,
            half_type,
            jax.ShapeDtypeStruct((SUB, width), jnp.float32),
        ),
        in_specs=[vmem, vmem, smem, smem],
        out_specs=(vmem,) * 4,
        scratch_shapes=[
            pltpu.VMEM((width, width), jnp.float32),
            pltpu.VMEM((pieces * piece_rows, LANES), jnp.float32),
            pltpu.VMEM((pieces * SUB, LANES), jnp.float32),
            pltpu.VMEM((LANES, LANES), jnp.float32),
            pltpu.VMEM((LANES, LANES), jnp.float32),
        ],
        compiler_params=pltpu.CompilerParams(vmem_limit_bytes=48 * 2**20),
    )(held, other, numbers, counts)


def whiten_kernel(x_ref, mean_ref, high_ref, low_ref, out_ref):
    width = x_ref.shape[1]
    high, low = split(x_ref[...] - mean_ref[:1, :])
    for right in range(0, width, TILE):
        here = slice(right, right + TILE)
        deep = slice(0, right + TILE)
        tile = fast_dot(high[:, deep], high_ref[here, deep], ((1,), (1,)))
        tile = tile + fast_dot(high[:, deep], low_ref[here, deep], ((1,), (1,)))
        out_ref[:, here] = tile + fast_dot(low[:, deep], high_ref[here, deep], ((1,), (1,)))


def whiten(embeddings, mean, high, low):
    rows, width = embeddings.shape
    whole = lambda i: (0, 0)
    return pl.pallas_call(
        whiten_kernel,
        grid=(rows // TILE,),
        out_shape=jax.ShapeDtypeStruct((rows, width), jnp.float32),
        in_specs=[
            pl.BlockSpec((TILE, width), lambda i: (i, 0)),
            pl.BlockSpec(mean.shape, whole),
            pl.BlockSpec((width, width), whole),
            pl.BlockSpec((width, width), whole),
        ],
        out_specs=pl.BlockSpec((TILE, width), lambda i: (i, 0)),
        compiler_params=pltpu.CompilerParams(vmem_limit_bytes=48 * 2**20),
    )(embeddings, mean, high, low)


def shards(embeddings):
    local_rows, width = embeddings.shape
    devices = lax.axis_size("grp") * lax.axis_size("wide")
    used = LANES * len(upper_blocks(width))
    piece_rows = -(-used // (SUB * devices)) * SUB
    packed, mean_rows = local_gram(embeddings, piece_rows * devices, SUB)
    held, other, numbers = sum_in_pieces(packed, mean_rows)
    factor, high, low, mean = factor_and_inverse(
        held, other, numbers, piece_rows, width, local_rows
    )
    return (whiten(embeddings, mean, high, low), factor)


def solution(mesh):
    rows = P(AXES, None)
    return jax.shard_map(
        shards,
        mesh=mesh,
        in_specs=(rows,),
        out_specs=(rows, P()),
        check_vma=False,
    )
```

```python
import jax
import jax.numpy as jnp
from jax import lax
from jax.experimental import pallas as pl
from jax.experimental.pallas import tpu as pltpu
from jax.sharding import PartitionSpec as P

AXES = ("grp", "wide")
LANES = 128
SUB = 8
TILE = 256
HIGHEST = lax.Precision.HIGHEST


def dot(a, b, dims):
    return lax.dot_general(
        a, b, (dims, ((), ())), precision=HIGHEST, preferred_element_type=jnp.float32
    )


def over_lanes(tile, lane):
    return jnp.broadcast_to(tile[:, lane : lane + 1], (SUB, LANES))


def over_rows(tile, row):
    return jnp.broadcast_to(tile[row : row + 1, :], (SUB, LANES))


def split(values):
    high = values.astype(jnp.bfloat16)
    return high, (values - high.astype(jnp.float32)).astype(jnp.bfloat16)


def fast_dot(a, b, dims):
    return lax.dot_general(a, b, (dims, ((), ())), preferred_element_type=jnp.float32)


def upper_blocks(width):
    n = width // LANES
    return [(i, j) for i in range(n) for j in range(i, n)]


def gram_kernel(x_ref, packed_ref, mean_ref, both_ref, swapped_ref):
    rows, width = x_ref.shape
    total = jnp.zeros((SUB, width), jnp.float32)
    for r in range(0, rows, LANES):
        part = x_ref[r : r + LANES, :]
        for q in range(0, LANES, SUB):
            total = total + part[q : q + SUB, :]
    mean = jnp.sum(total, axis=0, keepdims=True) * (1.0 / rows)
    for r in range(0, rows, LANES):
        high, low = split(x_ref[r : r + LANES, :] - mean)
        both_ref[r : r + LANES, :] = high
        both_ref[rows + r : rows + r + LANES, :] = low
        swapped_ref[r : r + LANES, :] = low
        swapped_ref[rows + r : rows + r + LANES, :] = high
    place = {block: LANES * p for p, block in enumerate(upper_blocks(width))}
    for left in range(0, width, TILE):
        turned = both_ref[:, left : left + TILE].T
        for right in range(left, width, TILE):
            here = slice(right, right + TILE)
            tile = fast_dot(turned, both_ref[:, here], ((1,), (0,)))
            tile = tile + fast_dot(turned, swapped_ref[:, here], ((1,), (0,)))
            for a in range(0, TILE, LANES):
                for b in range(0, TILE, LANES):
                    block = ((left + a) // LANES, (right + b) // LANES)
                    if block in place:
                        packed_ref[place[block] : place[block] + LANES, :] = tile[
                            a : a + LANES, b : b + LANES
                        ]
    used = LANES * len(place)
    if packed_ref.shape[0] > used:
        packed_ref[used:, :] = jnp.zeros((packed_ref.shape[0] - used, LANES), jnp.float32)
    mean_ref[...] = jnp.zeros(mean_ref.shape, jnp.float32)
    for b in range(width // LANES):
        mean_ref[b : b + 1, :] = mean[:, LANES * b : LANES * (b + 1)]


def local_gram(embeddings, packed_rows, mean_rows):
    rows, width = embeddings.shape
    return pl.pallas_call(
        gram_kernel,
        out_shape=(
            jax.ShapeDtypeStruct((packed_rows, LANES), jnp.float32),
            jax.ShapeDtypeStruct((mean_rows, LANES), jnp.float32),
        ),
        in_specs=[pl.BlockSpec(memory_space=pltpu.VMEM)],
        out_specs=(pl.BlockSpec(memory_space=pltpu.VMEM),) * 2,
        scratch_shapes=[pltpu.VMEM((2 * rows, width), jnp.bfloat16)] * 2,
        compiler_params=pltpu.CompilerParams(vmem_limit_bytes=48 * 2**20),
    )(embeddings)


def exchange_orders(bits):
    body = [b for b in (3, 1) + tuple(range(4, bits)) if b < bits]
    tail = [2] if bits > 2 else []
    return [0] + body + tail, [0] + body[-1:] + body[:-1] + tail


def sum_in_pieces(packed, mean_rows):
    devices = lax.axis_size("grp") * lax.axis_size("wide")
    bits = devices.bit_length() - 1
    orders = exchange_orders(bits)
    me = lax.axis_index(AXES)
    on_core = me & 1

    def partners(step):
        return [(d, d ^ (1 << orders[d & 1][step])) for d in range(devices)]

    def bit_at(step, core):
        return jnp.where(core == 0, me >> orders[0][step], me >> orders[1][step]) & 1

    mine, twin = on_core, 1 - on_core
    for step in range(1, bits):
        mine = mine * 2 + bit_at(step, on_core)
        twin = twin * 2 + bit_at(step, 1 - on_core)
    piece = packed
    for step in range(bits):
        bit = bit_at(step, on_core)
        half = piece.shape[0] // 2
        sent = lax.dynamic_slice_in_dim(piece, (1 - bit) * half, half, 0)
        kept = lax.dynamic_slice_in_dim(piece, bit * half, half, 0)
        piece = kept + lax.ppermute(sent, AXES, partners(step))
    held = jnp.concatenate([piece, mean_rows], axis=0)[None]
    for step in reversed(range(bits)):
        other = lax.ppermute(held, AXES, partners(step))
        if step:
            held = jnp.concatenate([held, other], axis=0)
    return held, other, jnp.stack([mine, twin])


def factor_block(block, upper_ref, inverse_ref):
    groups = LANES // SUB
    tiles = [block[SUB * p : SUB * (p + 1), :] for p in range(groups)]
    row_at = lax.broadcasted_iota(jnp.int32, (SUB, LANES), 0)
    lane_at = lax.broadcasted_iota(jnp.int32, (SUB, LANES), 1)
    unit = [
        jnp.where(lane_at == row_at + SUB * p, 1.0, 0.0).astype(jnp.float32)
        for p in range(groups)
    ]
    for g in range(groups):
        base = SUB * g
        ahead = g + 1 < groups
        rows = [over_rows(tiles[g], i) for i in range(SUB)]
        s = {
            (i, j): over_lanes(rows[i], base + j) for i in range(SUB) for j in range(i, SUB)
        }
        carried = [over_rows(unit[g], i) for i in range(SUB)]
        if ahead:
            column = [over_lanes(tiles[g + 1], base + i) for i in range(SUB)]
        scale = []
        for j in range(SUB):
            r = lax.rsqrt(s[j, j])
            scale.append(r)
            for k in range(j + 1, SUB):
                s[j, k] = s[j, k] * r
            for k in range(j + 1, SUB):
                for m in range(k, SUB):
                    s[k, m] = s[k, m] - s[j, k] * s[j, m]
            rows[j] = rows[j] * r
            carried[j] = carried[j] * r
            for k in range(j + 1, SUB):
                rows[k] = rows[k] - s[j, k] * rows[j]
                carried[k] = carried[k] - s[j, k] * carried[j]
            if ahead:
                column[j] = column[j] * r
                for k in range(j + 1, SUB):
                    column[k] = column[k] - column[j] * s[j, k]
                tiles[g + 1] = tiles[g + 1] - column[j] * rows[j]
                unit[g + 1] = unit[g + 1] - column[j] * carried[j]
            upper_ref[base + j : base + j + 1, :] = rows[j][:1, :]
            inverse_ref[base + j : base + j + 1, :] = carried[j][:1, :]
        if g + 2 < groups:
            for i in reversed(range(SUB)):
                for k in range(i + 1, SUB):
                    rows[i] = rows[i] - s[i, k] * rows[k]
                    carried[i] = carried[i] - s[i, k] * carried[k]
                rows[i] = rows[i] * scale[i]
                carried[i] = carried[i] * scale[i]
        for p in range(g + 2, groups):
            column = [over_lanes(tiles[p], base + i) for i in range(SUB)]
            tiles[p] = tiles[p] - tree_sum([c * x for c, x in zip(column, rows)])
            unit[p] = unit[p] - tree_sum([c * x for c, x in zip(column, carried)])
        yield


def tree_sum(terms):
    while len(terms) > 1:
        terms = [a + b for a, b in zip(terms[::2], terms[1::2])]
    return terms[0]


def in_three(values):
    high = values.astype(jnp.bfloat16)
    rest = values - high.astype(jnp.float32)
    middle = rest.astype(jnp.bfloat16)
    return high, middle, (rest - middle.astype(jnp.float32)).astype(jnp.bfloat16)


def left_parts(values):
    high, middle, low = in_three(values)
    return jnp.concatenate([high, middle], axis=1), jnp.concatenate([low, high], axis=1)


def right_parts(values):
    high, middle, low = in_three(values)
    stack = lambda a, b: jnp.concatenate([a, b], axis=0)
    return stack(high, high), stack(middle, middle), stack(high, low)


def parts_dot(left, right):
    plain = lambda a, b: fast_dot(a, b, ((1,), (0,)))
    return (plain(left[1], right[2]) + plain(left[0], right[1])) + plain(left[0], right[0])


def factor_kernel(
    held_ref,
    other_ref,
    numbers_ref,
    count_ref,
    factor_ref,
    high_ref,
    low_ref,
    mean_ref,
    work,
    packed,
    means_scr,
    upper_ref,
    inverse_ref,
):
    half = held_ref.shape[0]
    pieces = 2 * half
    width = factor_ref.shape[0]
    blocks = width // LANES
    piece_rows = packed.shape[0] // pieces

    for part, ref in enumerate((held_ref, other_ref)):

        def unpack(q, _):
            p = numbers_ref[part] ^ q
            to = pl.multiple_of(p * piece_rows, SUB)
            packed[pl.ds(to, piece_rows), :] = ref[q, :piece_rows, :]
            to = pl.multiple_of(p * SUB, SUB)
            means_scr[pl.ds(to, SUB), :] = ref[q, piece_rows : piece_rows + SUB, :]
            return 0

        lax.fori_loop(0, half, unpack, 0, unroll=True)

    stacked = means_scr[...].reshape(pieces, SUB, LANES)
    middle = jnp.mean(stacked, axis=0)
    apart = stacked - middle[None]
    wide = jnp.concatenate([apart[:, b, :] for b in range(blocks)], axis=1)
    for b in range(blocks):
        mean_ref[:, LANES * b : LANES * (b + 1)] = jnp.broadcast_to(
            middle[b : b + 1, :], (SUB, LANES)
        )
    total_scale = count_ref[1]
    place = {block: LANES * p for p, block in enumerate(upper_blocks(width))}
    span = lambda b, e=None: slice(LANES * b, LANES * (b + 1 if e is None else e))

    def gather(i, first, end):
        between = dot(wide[:, span(i)], wide[:, span(first, end)], ((0,), (0,)))
        for j in range(first, end):
            work[span(i), span(j)] = (
                packed[place[i, j] : place[i, j] + LANES, :]
                + between[:, span(j - first)] * count_ref[0]
            )

    def write_row(k):
        row_at = lax.broadcasted_iota(jnp.int32, (LANES, LANES), 0)
        col_at = lax.broadcasted_iota(jnp.int32, (LANES, LANES), 1)
        zero = jnp.zeros((LANES, LANES), jnp.float32)
        for j in range(blocks):
            if j < k:
                factor, back = zero, work[span(k), span(j)]
            elif j > k:
                factor, back = work[span(k), span(j)], zero
            else:
                factor = jnp.where(col_at >= row_at, upper_ref[k % 2], 0.0)
                back = inverse_ref[k % 2]
            factor_ref[span(k), span(j)] = factor * (1.0 / total_scale)
            high, low = split(back * total_scale)
            high_ref[span(k), span(j)] = high
            low_ref[span(k), span(j)] = low

    def below(k, i, left, right, first):
        change = parts_dot(left, [r[:, : LANES * (k + 1)] for r in right])
        if k:
            work[span(i), span(0, k)] = work[span(i), span(0, k)] - change[:, : LANES * k]
        work[span(i), span(k)] = -change[:, LANES * k :]
        if first < blocks:
            cols = span(first, blocks)
            work[span(i), cols] = work[span(i), cols] - parts_dot(
                left, [r[:, cols] for r in right]
            )

    def later(k, left, solved, turned):
        row = {}

        def solve_rest():
            if k:
                cols = span(0, k)
                work[span(k), cols] = parts_dot(left, right_parts(work[span(k), cols]))
            if k + 2 < blocks:
                cols = span(k + 2, blocks)
                work[span(k), cols] = parts_dot(left, right_parts(work[span(k), cols]))
            if k + 1 < blocks:
                work[span(k), span(k + 1)] = solved
            row["parts"] = right_parts(
                jnp.concatenate(
                    [
                        inverse_ref[k % 2] if j == k else work[span(k), span(j)]
                        for j in range(blocks)
                    ],
                    axis=1,
                )
            )

        todo = [solve_rest]
        for i in range(k + 1, blocks):

            def one(i=i):
                lead = turned if i == k + 1 else left_parts(work[span(k), span(i)].T)
                below(k, i, lead, row["parts"], max(i, k + 2))

            todo.append(one)
        todo.append(lambda: write_row(k))
        return todo

    gather(0, 0, 1)
    todo = [lambda: gather(0, 1, blocks)]
    todo += [lambda i=i: gather(i, i, blocks) for i in range(1, blocks)]
    for k in range(blocks):
        groups = LANES // SUB
        done = 0
        steps = factor_block(work[span(k), span(k)], upper_ref.at[k % 2], inverse_ref.at[k % 2])
        for g, _ in enumerate(steps):
            due = -(-len(todo) * (g + 1) // groups)
            for piece in todo[done:due]:
                piece()
            done = due
        left = left_parts(inverse_ref[k % 2])
        solved = turned = None
        if k + 1 < blocks:
            solved = parts_dot(left, right_parts(work[span(k), span(k + 1)]))
            turned = left_parts(solved.T)
            work[span(k + 1), span(k + 1)] = work[span(k + 1), span(k + 1)] - parts_dot(
                turned, right_parts(solved)
            )
        todo = later(k, left, solved, turned)
    for piece in todo:
        piece()


def factor_and_inverse(held, other, numbers, piece_rows, width, local_rows):
    pieces = 2 * held.shape[0]
    vmem = pl.BlockSpec(memory_space=pltpu.VMEM)
    smem = pl.BlockSpec(memory_space=pltpu.SMEM)
    half_type = jax.ShapeDtypeStruct((width, width), jnp.bfloat16)
    counts = jnp.array([local_rows, (local_rows * pieces) ** 0.5], jnp.float32)
    return pl.pallas_call(
        factor_kernel,
        out_shape=(
            jax.ShapeDtypeStruct((width, width), jnp.float32),
            half_type,
            half_type,
            jax.ShapeDtypeStruct((SUB, width), jnp.float32),
        ),
        in_specs=[vmem, vmem, smem, smem],
        out_specs=(vmem,) * 4,
        scratch_shapes=[
            pltpu.VMEM((width, width), jnp.float32),
            pltpu.VMEM((pieces * piece_rows, LANES), jnp.float32),
            pltpu.VMEM((pieces * SUB, LANES), jnp.float32),
            pltpu.VMEM((2, LANES, LANES), jnp.float32),
            pltpu.VMEM((2, LANES, LANES), jnp.float32),
        ],
        compiler_params=pltpu.CompilerParams(vmem_limit_bytes=48 * 2**20),
    )(held, other, numbers, counts)


def whiten_kernel(x_ref, mean_ref, high_ref, low_ref, out_ref):
    width = x_ref.shape[1]
    high, low = split(x_ref[...] - mean_ref[:1, :])
    for right in range(0, width, TILE):
        here = slice(right, right + TILE)
        deep = slice(0, right + TILE)
        tile = fast_dot(high[:, deep], high_ref[here, deep], ((1,), (1,)))
        tile = tile + fast_dot(high[:, deep], low_ref[here, deep], ((1,), (1,)))
        out_ref[:, here] = tile + fast_dot(low[:, deep], high_ref[here, deep], ((1,), (1,)))


def whiten(embeddings, mean, high, low):
    rows, width = embeddings.shape
    whole = lambda i: (0, 0)
    return pl.pallas_call(
        whiten_kernel,
        grid=(rows // TILE,),
        out_shape=jax.ShapeDtypeStruct((rows, width), jnp.float32),
        in_specs=[
            pl.BlockSpec((TILE, width), lambda i: (i, 0)),
            pl.BlockSpec(mean.shape, whole),
            pl.BlockSpec((width, width), whole),
            pl.BlockSpec((width, width), whole),
        ],
        out_specs=pl.BlockSpec((TILE, width), lambda i: (i, 0)),
        compiler_params=pltpu.CompilerParams(vmem_limit_bytes=48 * 2**20),
    )(embeddings, mean, high, low)


def shards(embeddings):
    local_rows, width = embeddings.shape
    devices = lax.axis_size("grp") * lax.axis_size("wide")
    used = LANES * len(upper_blocks(width))
    piece_rows = -(-used // (SUB * devices)) * SUB
    packed, mean_rows = local_gram(embeddings, piece_rows * devices, SUB)
    held, other, numbers = sum_in_pieces(packed, mean_rows)
    factor, high, low, mean = factor_and_inverse(
        held, other, numbers, piece_rows, width, local_rows
    )
    return (whiten(embeddings, mean, high, low), factor)


def solution(mesh):
    rows = P(AXES, None)
    return jax.shard_map(
        shards,
        mesh=mesh,
        in_specs=(rows,),
        out_specs=(rows, P()),
        check_vma=False,
    )
```

```python
import jax
import jax.numpy as jnp
from jax import lax
from jax.experimental import pallas as pl
from jax.experimental.pallas import tpu as pltpu
from jax.sharding import PartitionSpec as P

AXES = ("grp", "wide")
LANES = 128
SUB = 8
TILE = 256
HIGHEST = lax.Precision.HIGHEST


def dot(a, b, dims):
    return lax.dot_general(
        a, b, (dims, ((), ())), precision=HIGHEST, preferred_element_type=jnp.float32
    )


def over_lanes(tile, lane):
    return jnp.broadcast_to(tile[:, lane : lane + 1], (SUB, LANES))


def over_rows(tile, row):
    return jnp.broadcast_to(tile[row : row + 1, :], (SUB, LANES))


def split(values):
    high = values.astype(jnp.bfloat16)
    return high, (values - high.astype(jnp.float32)).astype(jnp.bfloat16)


def fast_dot(a, b, dims):
    return lax.dot_general(a, b, (dims, ((), ())), preferred_element_type=jnp.float32)


def upper_blocks(width):
    n = width // LANES
    return [(i, j) for i in range(n) for j in range(i, n)]


def gram_kernel(x_ref, packed_ref, mean_ref, both_ref, swapped_ref):
    rows, width = x_ref.shape
    total = jnp.zeros((SUB, width), jnp.float32)
    for r in range(0, rows, LANES):
        part = x_ref[r : r + LANES, :]
        for q in range(0, LANES, SUB):
            total = total + part[q : q + SUB, :]
    mean = jnp.sum(total, axis=0, keepdims=True) * (1.0 / rows)
    for r in range(0, rows, LANES):
        high, low = split(x_ref[r : r + LANES, :] - mean)
        both_ref[r : r + LANES, :] = high
        both_ref[rows + r : rows + r + LANES, :] = low
        swapped_ref[r : r + LANES, :] = low
        swapped_ref[rows + r : rows + r + LANES, :] = high
    place = {block: LANES * p for p, block in enumerate(upper_blocks(width))}
    for left in range(0, width, TILE):
        turned = both_ref[:, left : left + TILE].T
        for right in range(left, width, TILE):
            here = slice(right, right + TILE)
            tile = fast_dot(turned, both_ref[:, here], ((1,), (0,)))
            tile = tile + fast_dot(turned, swapped_ref[:, here], ((1,), (0,)))
            for a in range(0, TILE, LANES):
                for b in range(0, TILE, LANES):
                    block = ((left + a) // LANES, (right + b) // LANES)
                    if block in place:
                        packed_ref[place[block] : place[block] + LANES, :] = tile[
                            a : a + LANES, b : b + LANES
                        ]
    used = LANES * len(place)
    if packed_ref.shape[0] > used:
        packed_ref[used:, :] = jnp.zeros((packed_ref.shape[0] - used, LANES), jnp.float32)
    mean_ref[...] = jnp.zeros(mean_ref.shape, jnp.float32)
    for b in range(width // LANES):
        mean_ref[b : b + 1, :] = mean[:, LANES * b : LANES * (b + 1)]


def local_gram(embeddings, packed_rows, mean_rows):
    rows, width = embeddings.shape
    return pl.pallas_call(
        gram_kernel,
        out_shape=(
            jax.ShapeDtypeStruct((packed_rows, LANES), jnp.float32),
            jax.ShapeDtypeStruct((mean_rows, LANES), jnp.float32),
        ),
        in_specs=[pl.BlockSpec(memory_space=pltpu.VMEM)],
        out_specs=(pl.BlockSpec(memory_space=pltpu.VMEM),) * 2,
        scratch_shapes=[pltpu.VMEM((2 * rows, width), jnp.bfloat16)] * 2,
        compiler_params=pltpu.CompilerParams(vmem_limit_bytes=48 * 2**20),
    )(embeddings)


def sum_in_pieces(packed, mean_rows):
    groups, wide = lax.axis_size("grp"), lax.axis_size("wide")
    core = lax.axis_index("wide") & 1
    twins = [(d, d ^ 1) for d in range(wide)]
    same_core = [list(range(c, wide, 2)) for c in range(2)]

    def over_grp(parts):
        return lax.all_to_all(parts, "grp", 0, 0)

    def over_wide(parts):
        return lax.all_to_all(parts, "wide", 0, 0, axis_index_groups=same_core)

    def spread(parts, trade, count):
        return trade(jnp.broadcast_to(parts[None], (count,) + parts.shape))

    half = packed.shape[0] // 2
    sent = lax.dynamic_slice_in_dim(packed, (1 - core) * half, half, 0)
    kept = lax.dynamic_slice_in_dim(packed, core * half, half, 0)
    piece = kept + lax.ppermute(sent, "wide", twins)
    piece = jnp.sum(over_grp(piece.reshape(groups, -1, LANES)), axis=0)
    piece = jnp.sum(over_wide(piece.reshape(wide // 2, -1, LANES)), axis=0)
    held = jnp.concatenate([piece, mean_rows], axis=0)
    held = spread(held, over_wide, wide // 2)
    held = spread(held, over_grp, groups)
    held = held.reshape((-1,) + held.shape[2:])
    other = lax.ppermute(held, "wide", twins)
    half = held.shape[0]
    return held, other, jnp.stack([core * half, (1 - core) * half])


def factor_block(block, upper_ref, inverse_ref):
    groups = LANES // SUB
    tiles = [block[SUB * p : SUB * (p + 1), :] for p in range(groups)]
    row_at = lax.broadcasted_iota(jnp.int32, (SUB, LANES), 0)
    lane_at = lax.broadcasted_iota(jnp.int32, (SUB, LANES), 1)
    unit = [
        jnp.where(lane_at == row_at + SUB * p, 1.0, 0.0).astype(jnp.float32)
        for p in range(groups)
    ]
    for g in range(groups):
        base = SUB * g
        ahead = g + 1 < groups
        rows = [over_rows(tiles[g], i) for i in range(SUB)]
        s = {
            (i, j): over_lanes(rows[i], base + j) for i in range(SUB) for j in range(i, SUB)
        }
        carried = [over_rows(unit[g], i) for i in range(SUB)]
        if ahead:
            column = [over_lanes(tiles[g + 1], base + i) for i in range(SUB)]
        scale = []
        for j in range(SUB):
            r = lax.rsqrt(s[j, j])
            scale.append(r)
            for k in range(j + 1, SUB):
                s[j, k] = s[j, k] * r
            for k in range(j + 1, SUB):
                for m in range(k, SUB):
                    s[k, m] = s[k, m] - s[j, k] * s[j, m]
            rows[j] = rows[j] * r
            carried[j] = carried[j] * r
            for k in range(j + 1, SUB):
                rows[k] = rows[k] - s[j, k] * rows[j]
                carried[k] = carried[k] - s[j, k] * carried[j]
            if ahead:
                column[j] = column[j] * r
                for k in range(j + 1, SUB):
                    column[k] = column[k] - column[j] * s[j, k]
                tiles[g + 1] = tiles[g + 1] - column[j] * rows[j]
                unit[g + 1] = unit[g + 1] - column[j] * carried[j]
            upper_ref[base + j : base + j + 1, :] = rows[j][:1, :]
            inverse_ref[base + j : base + j + 1, :] = carried[j][:1, :]
        if g + 2 < groups:
            for i in reversed(range(SUB)):
                for k in range(i + 1, SUB):
                    rows[i] = rows[i] - s[i, k] * rows[k]
                    carried[i] = carried[i] - s[i, k] * carried[k]
                rows[i] = rows[i] * scale[i]
                carried[i] = carried[i] * scale[i]
        for p in range(g + 2, groups):
            column = [over_lanes(tiles[p], base + i) for i in range(SUB)]
            tiles[p] = tiles[p] - tree_sum([c * x for c, x in zip(column, rows)])
            unit[p] = unit[p] - tree_sum([c * x for c, x in zip(column, carried)])
        yield


def tree_sum(terms):
    while len(terms) > 1:
        terms = [a + b for a, b in zip(terms[::2], terms[1::2])]
    return terms[0]


def in_three(values):
    high = values.astype(jnp.bfloat16)
    rest = values - high.astype(jnp.float32)
    middle = rest.astype(jnp.bfloat16)
    return high, middle, (rest - middle.astype(jnp.float32)).astype(jnp.bfloat16)


def left_parts(values):
    high, middle, low = in_three(values)
    return jnp.concatenate([high, middle], axis=1), jnp.concatenate([low, high], axis=1)


def right_parts(values):
    high, middle, low = in_three(values)
    stack = lambda a, b: jnp.concatenate([a, b], axis=0)
    return stack(high, high), stack(middle, middle), stack(high, low)


def parts_dot(left, right):
    plain = lambda a, b: fast_dot(a, b, ((1,), (0,)))
    return (plain(left[1], right[2]) + plain(left[0], right[1])) + plain(left[0], right[0])


def factor_kernel(
    held_ref,
    other_ref,
    numbers_ref,
    count_ref,
    factor_ref,
    high_ref,
    low_ref,
    mean_ref,
    work,
    packed,
    means_scr,
    upper_ref,
    inverse_ref,
):
    half = held_ref.shape[0]
    pieces = 2 * half
    width = factor_ref.shape[0]
    blocks = width // LANES
    piece_rows = packed.shape[0] // pieces

    for part, ref in enumerate((held_ref, other_ref)):

        def unpack(q, _):
            p = numbers_ref[part] ^ q
            to = pl.multiple_of(p * piece_rows, SUB)
            packed[pl.ds(to, piece_rows), :] = ref[q, :piece_rows, :]
            to = pl.multiple_of(p * SUB, SUB)
            means_scr[pl.ds(to, SUB), :] = ref[q, piece_rows : piece_rows + SUB, :]
            return 0

        lax.fori_loop(0, half, unpack, 0, unroll=True)

    stacked = means_scr[...].reshape(pieces, SUB, LANES)
    middle = jnp.mean(stacked, axis=0)
    apart = stacked - middle[None]
    wide = jnp.concatenate([apart[:, b, :] for b in range(blocks)], axis=1)
    for b in range(blocks):
        mean_ref[:, LANES * b : LANES * (b + 1)] = jnp.broadcast_to(
            middle[b : b + 1, :], (SUB, LANES)
        )
    total_scale = count_ref[1]
    place = {block: LANES * p for p, block in enumerate(upper_blocks(width))}
    span = lambda b, e=None: slice(LANES * b, LANES * (b + 1 if e is None else e))

    def gather(i, first, end):
        between = dot(wide[:, span(i)], wide[:, span(first, end)], ((0,), (0,)))
        for j in range(first, end):
            work[span(i), span(j)] = (
                packed[place[i, j] : place[i, j] + LANES, :]
                + between[:, span(j - first)] * count_ref[0]
            )

    def write_row(k):
        row_at = lax.broadcasted_iota(jnp.int32, (LANES, LANES), 0)
        col_at = lax.broadcasted_iota(jnp.int32, (LANES, LANES), 1)
        zero = jnp.zeros((LANES, LANES), jnp.float32)
        for j in range(blocks):
            if j < k:
                factor, back = zero, work[span(k), span(j)]
            elif j > k:
                factor, back = work[span(k), span(j)], zero
            else:
                factor = jnp.where(col_at >= row_at, upper_ref[k % 2], 0.0)
                back = inverse_ref[k % 2]
            factor_ref[span(k), span(j)] = factor * (1.0 / total_scale)
            high, low = split(back * total_scale)
            high_ref[span(k), span(j)] = high
            low_ref[span(k), span(j)] = low

    def below(k, i, left, right, first):
        change = parts_dot(left, [r[:, : LANES * (k + 1)] for r in right])
        if k:
            work[span(i), span(0, k)] = work[span(i), span(0, k)] - change[:, : LANES * k]
        work[span(i), span(k)] = -change[:, LANES * k :]
        if first < blocks:
            cols = span(first, blocks)
            work[span(i), cols] = work[span(i), cols] - parts_dot(
                left, [r[:, cols] for r in right]
            )

    def later(k, left, solved, turned):
        row = {}

        def solve_rest():
            if k:
                cols = span(0, k)
                work[span(k), cols] = parts_dot(left, right_parts(work[span(k), cols]))
            if k + 2 < blocks:
                cols = span(k + 2, blocks)
                work[span(k), cols] = parts_dot(left, right_parts(work[span(k), cols]))
            if k + 1 < blocks:
                work[span(k), span(k + 1)] = solved
            row["parts"] = right_parts(
                jnp.concatenate(
                    [
                        inverse_ref[k % 2] if j == k else work[span(k), span(j)]
                        for j in range(blocks)
                    ],
                    axis=1,
                )
            )

        todo = [solve_rest]
        for i in range(k + 1, blocks):

            def one(i=i):
                lead = turned if i == k + 1 else left_parts(work[span(k), span(i)].T)
                below(k, i, lead, row["parts"], max(i, k + 2))

            todo.append(one)
        todo.append(lambda: write_row(k))
        return todo

    gather(0, 0, 1)
    todo = [lambda: gather(0, 1, blocks)]
    todo += [lambda i=i: gather(i, i, blocks) for i in range(1, blocks)]
    for k in range(blocks):
        groups = LANES // SUB
        done = 0
        steps = factor_block(work[span(k), span(k)], upper_ref.at[k % 2], inverse_ref.at[k % 2])
        for g, _ in enumerate(steps):
            due = -(-len(todo) * (g + 1) // groups)
            for piece in todo[done:due]:
                piece()
            done = due
        left = left_parts(inverse_ref[k % 2])
        solved = turned = None
        if k + 1 < blocks:
            solved = parts_dot(left, right_parts(work[span(k), span(k + 1)]))
            turned = left_parts(solved.T)
            work[span(k + 1), span(k + 1)] = work[span(k + 1), span(k + 1)] - parts_dot(
                turned, right_parts(solved)
            )
        todo = later(k, left, solved, turned)
    for piece in todo:
        piece()


def factor_and_inverse(held, other, numbers, piece_rows, width, local_rows):
    pieces = 2 * held.shape[0]
    vmem = pl.BlockSpec(memory_space=pltpu.VMEM)
    smem = pl.BlockSpec(memory_space=pltpu.SMEM)
    half_type = jax.ShapeDtypeStruct((width, width), jnp.bfloat16)
    counts = jnp.array([local_rows, (local_rows * pieces) ** 0.5], jnp.float32)
    return pl.pallas_call(
        factor_kernel,
        out_shape=(
            jax.ShapeDtypeStruct((width, width), jnp.float32),
            half_type,
            half_type,
            jax.ShapeDtypeStruct((SUB, width), jnp.float32),
        ),
        in_specs=[vmem, vmem, smem, smem],
        out_specs=(vmem,) * 4,
        scratch_shapes=[
            pltpu.VMEM((width, width), jnp.float32),
            pltpu.VMEM((pieces * piece_rows, LANES), jnp.float32),
            pltpu.VMEM((pieces * SUB, LANES), jnp.float32),
            pltpu.VMEM((2, LANES, LANES), jnp.float32),
            pltpu.VMEM((2, LANES, LANES), jnp.float32),
        ],
        compiler_params=pltpu.CompilerParams(vmem_limit_bytes=48 * 2**20),
    )(held, other, numbers, counts)


def whiten_kernel(x_ref, mean_ref, high_ref, low_ref, out_ref):
    width = x_ref.shape[1]
    high, low = split(x_ref[...] - mean_ref[:1, :])
    for right in range(0, width, TILE):
        here = slice(right, right + TILE)
        deep = slice(0, right + TILE)
        tile = fast_dot(high[:, deep], high_ref[here, deep], ((1,), (1,)))
        tile = tile + fast_dot(high[:, deep], low_ref[here, deep], ((1,), (1,)))
        out_ref[:, here] = tile + fast_dot(low[:, deep], high_ref[here, deep], ((1,), (1,)))


def whiten(embeddings, mean, high, low):
    rows, width = embeddings.shape
    whole = lambda i: (0, 0)
    return pl.pallas_call(
        whiten_kernel,
        grid=(rows // TILE,),
        out_shape=jax.ShapeDtypeStruct((rows, width), jnp.float32),
        in_specs=[
            pl.BlockSpec((TILE, width), lambda i: (i, 0)),
            pl.BlockSpec(mean.shape, whole),
            pl.BlockSpec((width, width), whole),
            pl.BlockSpec((width, width), whole),
        ],
        out_specs=pl.BlockSpec((TILE, width), lambda i: (i, 0)),
        compiler_params=pltpu.CompilerParams(vmem_limit_bytes=48 * 2**20),
    )(embeddings, mean, high, low)


def shards(embeddings):
    local_rows, width = embeddings.shape
    devices = lax.axis_size("grp") * lax.axis_size("wide")
    used = LANES * len(upper_blocks(width))
    piece_rows = -(-used // (SUB * devices)) * SUB
    packed, mean_rows = local_gram(embeddings, piece_rows * devices, SUB)
    held, other, numbers = sum_in_pieces(packed, mean_rows)
    factor, high, low, mean = factor_and_inverse(
        held, other, numbers, piece_rows, width, local_rows
    )
    return (whiten(embeddings, mean, high, low), factor)


def solution(mesh):
    rows = P(AXES, None)
    return jax.shard_map(
        shards,
        mesh=mesh,
        in_specs=(rows,),
        out_specs=(rows, P()),
        check_vma=False,
    )
```

```python
import jax
import jax.numpy as jnp
from jax import lax
from jax.experimental import pallas as pl
from jax.experimental.pallas import tpu as pltpu
from jax.sharding import PartitionSpec as P

AXES = ("grp", "wide")
LANES = 128
SUB = 8
TILE = 256
HIGHEST = lax.Precision.HIGHEST


def dot(a, b, dims):
    return lax.dot_general(
        a, b, (dims, ((), ())), precision=HIGHEST, preferred_element_type=jnp.float32
    )


def over_lanes(tile, lane):
    return jnp.broadcast_to(tile[:, lane : lane + 1], (SUB, LANES))


def over_rows(tile, row):
    return jnp.broadcast_to(tile[row : row + 1, :], (SUB, LANES))


def split(values):
    high = values.astype(jnp.bfloat16)
    return high, (values - high.astype(jnp.float32)).astype(jnp.bfloat16)


def fast_dot(a, b, dims):
    return lax.dot_general(a, b, (dims, ((), ())), preferred_element_type=jnp.float32)


def upper_blocks(width):
    n = width // LANES
    return [(i, j) for i in range(n) for j in range(i, n)]


def gram_kernel(x_ref, packed_ref, mean_ref, both_ref, swapped_ref):
    rows, width = x_ref.shape
    total = jnp.zeros((SUB, width), jnp.float32)
    for r in range(0, rows, LANES):
        part = x_ref[r : r + LANES, :]
        for q in range(0, LANES, SUB):
            total = total + part[q : q + SUB, :]
    mean = jnp.sum(total, axis=0, keepdims=True) * (1.0 / rows)
    for r in range(0, rows, LANES):
        high, low = split(x_ref[r : r + LANES, :] - mean)
        both_ref[r : r + LANES, :] = high
        both_ref[rows + r : rows + r + LANES, :] = low
        swapped_ref[r : r + LANES, :] = low
        swapped_ref[rows + r : rows + r + LANES, :] = high
    place = {block: LANES * p for p, block in enumerate(upper_blocks(width))}
    for left in range(0, width, TILE):
        turned = both_ref[:, left : left + TILE].T
        for right in range(left, width, TILE):
            here = slice(right, right + TILE)
            tile = fast_dot(turned, both_ref[:, here], ((1,), (0,)))
            tile = tile + fast_dot(turned, swapped_ref[:, here], ((1,), (0,)))
            for a in range(0, TILE, LANES):
                for b in range(0, TILE, LANES):
                    block = ((left + a) // LANES, (right + b) // LANES)
                    if block in place:
                        packed_ref[place[block] : place[block] + LANES, :] = tile[
                            a : a + LANES, b : b + LANES
                        ]
    used = LANES * len(place)
    if packed_ref.shape[0] > used:
        packed_ref[used:, :] = jnp.zeros((packed_ref.shape[0] - used, LANES), jnp.float32)
    mean_ref[...] = jnp.zeros(mean_ref.shape, jnp.float32)
    for b in range(width // LANES):
        mean_ref[b : b + 1, :] = mean[:, LANES * b : LANES * (b + 1)]


def local_gram(embeddings, packed_rows, mean_rows):
    rows, width = embeddings.shape
    return pl.pallas_call(
        gram_kernel,
        out_shape=(
            jax.ShapeDtypeStruct((packed_rows, LANES), jnp.float32),
            jax.ShapeDtypeStruct((mean_rows, LANES), jnp.float32),
        ),
        in_specs=[pl.BlockSpec(memory_space=pltpu.VMEM)],
        out_specs=(pl.BlockSpec(memory_space=pltpu.VMEM),) * 2,
        scratch_shapes=[pltpu.VMEM((2 * rows, width), jnp.bfloat16)] * 2,
        compiler_params=pltpu.CompilerParams(vmem_limit_bytes=48 * 2**20),
    )(embeddings)


def exchange_orders(bits):
    body = [b for b in (3, 1) + tuple(range(4, bits)) if b < bits]
    tail = [2] if bits > 2 else []
    return [0] + body + tail, [0] + body[-1:] + body[:-1] + tail


def sum_in_pieces(packed, mean_rows):
    groups, wide = lax.axis_size("grp"), lax.axis_size("wide")
    devices = groups * wide
    bits = devices.bit_length() - 1
    orders = exchange_orders(bits)
    me = lax.axis_index(AXES)
    core = me & 1
    twins = [(d, d ^ 1) for d in range(wide)]
    same_core = [list(range(c, wide, 2)) for c in range(2)]

    def number(device):
        order = orders[device & 1]
        return sum(((device >> b) & 1) << (bits - 1 - step) for step, b in enumerate(order))

    piece = packed
    for step in range(bits):
        bit = jnp.where(core == 0, me >> orders[0][step], me >> orders[1][step]) & 1
        half = piece.shape[0] // 2
        sent = lax.dynamic_slice_in_dim(piece, (1 - bit) * half, half, 0)
        kept = lax.dynamic_slice_in_dim(piece, bit * half, half, 0)
        to = [(d, d ^ (1 << orders[d & 1][step])) for d in range(devices)]
        piece = kept + lax.ppermute(sent, AXES, to)
    held = jnp.concatenate([piece, mean_rows], axis=0)
    held = jnp.broadcast_to(held[None], (wide // 2,) + held.shape)
    held = lax.all_to_all(held, "wide", 0, 0, axis_index_groups=same_core)
    held = jnp.broadcast_to(held[None], (groups,) + held.shape)
    held = lax.all_to_all(held, "grp", 0, 0)
    held = held.reshape((-1,) + held.shape[2:])
    other = lax.ppermute(held, "wide", twins)
    even, odd = ([number(d) for d in range(c, devices, 2)] for c in range(2))
    numbers = jnp.where(
        core == 0, jnp.array(even + odd, jnp.int32), jnp.array(odd + even, jnp.int32)
    )
    return held, other, numbers


def factor_block(block, upper_ref, inverse_ref):
    groups = LANES // SUB
    tiles = [block[SUB * p : SUB * (p + 1), :] for p in range(groups)]
    row_at = lax.broadcasted_iota(jnp.int32, (SUB, LANES), 0)
    lane_at = lax.broadcasted_iota(jnp.int32, (SUB, LANES), 1)
    unit = [
        jnp.where(lane_at == row_at + SUB * p, 1.0, 0.0).astype(jnp.float32)
        for p in range(groups)
    ]
    for g in range(groups):
        base = SUB * g
        ahead = g + 1 < groups
        rows = [over_rows(tiles[g], i) for i in range(SUB)]
        s = {
            (i, j): over_lanes(rows[i], base + j) for i in range(SUB) for j in range(i, SUB)
        }
        carried = [over_rows(unit[g], i) for i in range(SUB)]
        if ahead:
            column = [over_lanes(tiles[g + 1], base + i) for i in range(SUB)]
        scale = []
        for j in range(SUB):
            r = lax.rsqrt(s[j, j])
            scale.append(r)
            for k in range(j + 1, SUB):
                s[j, k] = s[j, k] * r
            for k in range(j + 1, SUB):
                for m in range(k, SUB):
                    s[k, m] = s[k, m] - s[j, k] * s[j, m]
            rows[j] = rows[j] * r
            carried[j] = carried[j] * r
            for k in range(j + 1, SUB):
                rows[k] = rows[k] - s[j, k] * rows[j]
                carried[k] = carried[k] - s[j, k] * carried[j]
            if ahead:
                column[j] = column[j] * r
                for k in range(j + 1, SUB):
                    column[k] = column[k] - column[j] * s[j, k]
                tiles[g + 1] = tiles[g + 1] - column[j] * rows[j]
                unit[g + 1] = unit[g + 1] - column[j] * carried[j]
            upper_ref[base + j : base + j + 1, :] = rows[j][:1, :]
            inverse_ref[base + j : base + j + 1, :] = carried[j][:1, :]
        if g + 2 < groups:
            for i in reversed(range(SUB)):
                for k in range(i + 1, SUB):
                    rows[i] = rows[i] - s[i, k] * rows[k]
                    carried[i] = carried[i] - s[i, k] * carried[k]
                rows[i] = rows[i] * scale[i]
                carried[i] = carried[i] * scale[i]
        for p in range(g + 2, groups):
            column = [over_lanes(tiles[p], base + i) for i in range(SUB)]
            tiles[p] = tiles[p] - tree_sum([c * x for c, x in zip(column, rows)])
            unit[p] = unit[p] - tree_sum([c * x for c, x in zip(column, carried)])
        yield


def tree_sum(terms):
    while len(terms) > 1:
        terms = [a + b for a, b in zip(terms[::2], terms[1::2])]
    return terms[0]


def in_three(values):
    high = values.astype(jnp.bfloat16)
    rest = values - high.astype(jnp.float32)
    middle = rest.astype(jnp.bfloat16)
    return high, middle, (rest - middle.astype(jnp.float32)).astype(jnp.bfloat16)


def left_parts(values):
    high, middle, low = in_three(values)
    return jnp.concatenate([high, middle], axis=1), jnp.concatenate([low, high], axis=1)


def right_parts(values):
    high, middle, low = in_three(values)
    stack = lambda a, b: jnp.concatenate([a, b], axis=0)
    return stack(high, high), stack(middle, middle), stack(high, low)


def parts_dot(left, right):
    plain = lambda a, b: fast_dot(a, b, ((1,), (0,)))
    return (plain(left[1], right[2]) + plain(left[0], right[1])) + plain(left[0], right[0])


def factor_kernel(
    held_ref,
    other_ref,
    numbers_ref,
    count_ref,
    factor_ref,
    high_ref,
    low_ref,
    mean_ref,
    work,
    packed,
    means_scr,
    upper_ref,
    inverse_ref,
):
    half = held_ref.shape[0]
    pieces = 2 * half
    width = factor_ref.shape[0]
    blocks = width // LANES
    piece_rows = packed.shape[0] // pieces

    for part, ref in enumerate((held_ref, other_ref)):

        def unpack(q, _):
            p = numbers_ref[part * half + q]
            to = pl.multiple_of(p * piece_rows, SUB)
            packed[pl.ds(to, piece_rows), :] = ref[q, :piece_rows, :]
            to = pl.multiple_of(p * SUB, SUB)
            means_scr[pl.ds(to, SUB), :] = ref[q, piece_rows : piece_rows + SUB, :]
            return 0

        lax.fori_loop(0, half, unpack, 0, unroll=True)

    stacked = means_scr[...].reshape(pieces, SUB, LANES)
    middle = jnp.mean(stacked, axis=0)
    apart = stacked - middle[None]
    wide = jnp.concatenate([apart[:, b, :] for b in range(blocks)], axis=1)
    for b in range(blocks):
        mean_ref[:, LANES * b : LANES * (b + 1)] = jnp.broadcast_to(
            middle[b : b + 1, :], (SUB, LANES)
        )
    total_scale = count_ref[1]
    place = {block: LANES * p for p, block in enumerate(upper_blocks(width))}
    span = lambda b, e=None: slice(LANES * b, LANES * (b + 1 if e is None else e))

    def gather(i, first, end):
        between = dot(wide[:, span(i)], wide[:, span(first, end)], ((0,), (0,)))
        for j in range(first, end):
            work[span(i), span(j)] = (
                packed[place[i, j] : place[i, j] + LANES, :]
                + between[:, span(j - first)] * count_ref[0]
            )

    def write_row(k):
        row_at = lax.broadcasted_iota(jnp.int32, (LANES, LANES), 0)
        col_at = lax.broadcasted_iota(jnp.int32, (LANES, LANES), 1)
        zero = jnp.zeros((LANES, LANES), jnp.float32)
        for j in range(blocks):
            if j < k:
                factor, back = zero, work[span(k), span(j)]
            elif j > k:
                factor, back = work[span(k), span(j)], zero
            else:
                factor = jnp.where(col_at >= row_at, upper_ref[k % 2], 0.0)
                back = inverse_ref[k % 2]
            factor_ref[span(k), span(j)] = factor * (1.0 / total_scale)
            high, low = split(back * total_scale)
            high_ref[span(k), span(j)] = high
            low_ref[span(k), span(j)] = low

    def below(k, i, left, right, first):
        change = parts_dot(left, [r[:, : LANES * (k + 1)] for r in right])
        if k:
            work[span(i), span(0, k)] = work[span(i), span(0, k)] - change[:, : LANES * k]
        work[span(i), span(k)] = -change[:, LANES * k :]
        if first < blocks:
            cols = span(first, blocks)
            work[span(i), cols] = work[span(i), cols] - parts_dot(
                left, [r[:, cols] for r in right]
            )

    def later(k, left, solved, turned):
        row = {}

        def solve_rest():
            if k:
                cols = span(0, k)
                work[span(k), cols] = parts_dot(left, right_parts(work[span(k), cols]))
            if k + 2 < blocks:
                cols = span(k + 2, blocks)
                work[span(k), cols] = parts_dot(left, right_parts(work[span(k), cols]))
            if k + 1 < blocks:
                work[span(k), span(k + 1)] = solved
            row["parts"] = right_parts(
                jnp.concatenate(
                    [
                        inverse_ref[k % 2] if j == k else work[span(k), span(j)]
                        for j in range(blocks)
                    ],
                    axis=1,
                )
            )

        todo = [solve_rest]
        for i in range(k + 1, blocks):

            def one(i=i):
                lead = turned if i == k + 1 else left_parts(work[span(k), span(i)].T)
                below(k, i, lead, row["parts"], max(i, k + 2))

            todo.append(one)
        todo.append(lambda: write_row(k))
        return todo

    gather(0, 0, 1)
    todo = [lambda: gather(0, 1, blocks)]
    todo += [lambda i=i: gather(i, i, blocks) for i in range(1, blocks)]
    for k in range(blocks):
        groups = LANES // SUB
        done = 0
        steps = factor_block(work[span(k), span(k)], upper_ref.at[k % 2], inverse_ref.at[k % 2])
        for g, _ in enumerate(steps):
            due = -(-len(todo) * (g + 1) // groups)
            for piece in todo[done:due]:
                piece()
            done = due
        left = left_parts(inverse_ref[k % 2])
        solved = turned = None
        if k + 1 < blocks:
            solved = parts_dot(left, right_parts(work[span(k), span(k + 1)]))
            turned = left_parts(solved.T)
            work[span(k + 1), span(k + 1)] = work[span(k + 1), span(k + 1)] - parts_dot(
                turned, right_parts(solved)
            )
        todo = later(k, left, solved, turned)
    for piece in todo:
        piece()


def factor_and_inverse(held, other, numbers, piece_rows, width, local_rows):
    pieces = 2 * held.shape[0]
    vmem = pl.BlockSpec(memory_space=pltpu.VMEM)
    smem = pl.BlockSpec(memory_space=pltpu.SMEM)
    half_type = jax.ShapeDtypeStruct((width, width), jnp.bfloat16)
    counts = jnp.array([local_rows, (local_rows * pieces) ** 0.5], jnp.float32)
    return pl.pallas_call(
        factor_kernel,
        out_shape=(
            jax.ShapeDtypeStruct((width, width), jnp.float32),
            half_type,
            half_type,
            jax.ShapeDtypeStruct((SUB, width), jnp.float32),
        ),
        in_specs=[vmem, vmem, smem, smem],
        out_specs=(vmem,) * 4,
        scratch_shapes=[
            pltpu.VMEM((width, width), jnp.float32),
            pltpu.VMEM((pieces * piece_rows, LANES), jnp.float32),
            pltpu.VMEM((pieces * SUB, LANES), jnp.float32),
            pltpu.VMEM((2, LANES, LANES), jnp.float32),
            pltpu.VMEM((2, LANES, LANES), jnp.float32),
        ],
        compiler_params=pltpu.CompilerParams(vmem_limit_bytes=48 * 2**20),
    )(held, other, numbers, counts)


def whiten_kernel(x_ref, mean_ref, high_ref, low_ref, out_ref):
    width = x_ref.shape[1]
    high, low = split(x_ref[...] - mean_ref[:1, :])
    for right in range(0, width, TILE):
        here = slice(right, right + TILE)
        deep = slice(0, right + TILE)
        tile = fast_dot(high[:, deep], high_ref[here, deep], ((1,), (1,)))
        tile = tile + fast_dot(high[:, deep], low_ref[here, deep], ((1,), (1,)))
        out_ref[:, here] = tile + fast_dot(low[:, deep], high_ref[here, deep], ((1,), (1,)))


def whiten(embeddings, mean, high, low):
    rows, width = embeddings.shape
    whole = lambda i: (0, 0)
    return pl.pallas_call(
        whiten_kernel,
        grid=(rows // TILE,),
        out_shape=jax.ShapeDtypeStruct((rows, width), jnp.float32),
        in_specs=[
            pl.BlockSpec((TILE, width), lambda i: (i, 0)),
            pl.BlockSpec(mean.shape, whole),
            pl.BlockSpec((width, width), whole),
            pl.BlockSpec((width, width), whole),
        ],
        out_specs=pl.BlockSpec((TILE, width), lambda i: (i, 0)),
        compiler_params=pltpu.CompilerParams(vmem_limit_bytes=48 * 2**20),
    )(embeddings, mean, high, low)


def shards(embeddings):
    local_rows, width = embeddings.shape
    devices = lax.axis_size("grp") * lax.axis_size("wide")
    used = LANES * len(upper_blocks(width))
    piece_rows = -(-used // (SUB * devices)) * SUB
    packed, mean_rows = local_gram(embeddings, piece_rows * devices, SUB)
    held, other, numbers = sum_in_pieces(packed, mean_rows)
    factor, high, low, mean = factor_and_inverse(
        held, other, numbers, piece_rows, width, local_rows
    )
    return (whiten(embeddings, mean, high, low), factor)


def solution(mesh):
    rows = P(AXES, None)
    return jax.shard_map(
        shards,
        mesh=mesh,
        in_specs=(rows,),
        out_specs=(rows, P()),
        check_vma=False,
    )
```

```python
import jax
import jax.numpy as jnp
from jax import lax
from jax.experimental import pallas as pl
from jax.experimental.pallas import tpu as pltpu
from jax.sharding import PartitionSpec as P

AXES = ("grp", "wide")
LANES = 128
SUB = 8
TILE = 256
HIGHEST = lax.Precision.HIGHEST


def dot(a, b, dims):
    return lax.dot_general(
        a, b, (dims, ((), ())), precision=HIGHEST, preferred_element_type=jnp.float32
    )


def over_lanes(tile, lane):
    return jnp.broadcast_to(tile[:, lane : lane + 1], (SUB, LANES))


def over_rows(tile, row):
    return jnp.broadcast_to(tile[row : row + 1, :], (SUB, LANES))


def split(values):
    high = values.astype(jnp.bfloat16)
    return high, (values - high.astype(jnp.float32)).astype(jnp.bfloat16)


def fast_dot(a, b, dims):
    return lax.dot_general(a, b, (dims, ((), ())), preferred_element_type=jnp.float32)


def upper_blocks(width):
    n = width // LANES
    return [(i, j) for i in range(n) for j in range(i, n)]


def chunk_copies(source, target, arrived):
    return [
        pltpu.make_async_copy(
            source.at[pl.ds(r, TILE), :], target.at[pl.ds(r, TILE), :], arrived.at[r // TILE]
        )
        for r in range(0, source.shape[0], TILE)
    ]


def gram_kernel(x_hbm, packed_ref, mean_ref, x_ref, both_ref, swapped_ref, arrived):
    rows, width = x_ref.shape
    copies = chunk_copies(x_hbm, x_ref, arrived)
    for copy in copies:
        copy.start()
    total = jnp.zeros((SUB, width), jnp.float32)
    for r in range(0, rows, LANES):
        if r % TILE == 0:
            copies[r // TILE].wait()
        part = x_ref[r : r + LANES, :]
        for q in range(0, LANES, SUB):
            total = total + part[q : q + SUB, :]
    mean = jnp.sum(total, axis=0, keepdims=True) * (1.0 / rows)
    for r in range(0, rows, LANES):
        high, low = split(x_ref[r : r + LANES, :] - mean)
        both_ref[r : r + LANES, :] = high
        both_ref[rows + r : rows + r + LANES, :] = low
        swapped_ref[r : r + LANES, :] = low
        swapped_ref[rows + r : rows + r + LANES, :] = high
    place = {block: LANES * p for p, block in enumerate(upper_blocks(width))}
    for left in range(0, width, TILE):
        turned = both_ref[:, left : left + TILE].T
        for right in range(left, width, TILE):
            here = slice(right, right + TILE)
            tile = fast_dot(turned, both_ref[:, here], ((1,), (0,)))
            tile = tile + fast_dot(turned, swapped_ref[:, here], ((1,), (0,)))
            for a in range(0, TILE, LANES):
                for b in range(0, TILE, LANES):
                    block = ((left + a) // LANES, (right + b) // LANES)
                    if block in place:
                        packed_ref[place[block] : place[block] + LANES, :] = tile[
                            a : a + LANES, b : b + LANES
                        ]
    used = LANES * len(place)
    if packed_ref.shape[0] > used:
        packed_ref[used:, :] = jnp.zeros((packed_ref.shape[0] - used, LANES), jnp.float32)
    mean_ref[...] = jnp.zeros(mean_ref.shape, jnp.float32)
    for b in range(width // LANES):
        mean_ref[b : b + 1, :] = mean[:, LANES * b : LANES * (b + 1)]


def local_gram(embeddings, packed_rows, mean_rows):
    rows, width = embeddings.shape
    return pl.pallas_call(
        gram_kernel,
        out_shape=(
            jax.ShapeDtypeStruct((packed_rows, LANES), jnp.float32),
            jax.ShapeDtypeStruct((mean_rows, LANES), jnp.float32),
        ),
        in_specs=[pl.BlockSpec(memory_space=pl.ANY)],
        out_specs=(pl.BlockSpec(memory_space=pltpu.VMEM),) * 2,
        scratch_shapes=[pltpu.VMEM((rows, width), jnp.float32)]
        + [pltpu.VMEM((2 * rows, width), jnp.bfloat16)] * 2
        + [pltpu.SemaphoreType.DMA((rows // TILE,))],
        compiler_params=pltpu.CompilerParams(vmem_limit_bytes=48 * 2**20),
    )(embeddings)


def sum_in_pieces(packed, mean_rows):
    groups, wide = lax.axis_size("grp"), lax.axis_size("wide")
    core = lax.axis_index("wide") & 1
    twins = [(d, d ^ 1) for d in range(wide)]
    same_core = [list(range(c, wide, 2)) for c in range(2)]

    def over_grp(parts):
        return lax.all_to_all(parts, "grp", 0, 0)

    def over_wide(parts):
        return lax.all_to_all(parts, "wide", 0, 0, axis_index_groups=same_core)

    def spread(parts, trade, count):
        return trade(jnp.broadcast_to(parts[None], (count,) + parts.shape))

    half = packed.shape[0] // 2
    sent = lax.dynamic_slice_in_dim(packed, (1 - core) * half, half, 0)
    kept = lax.dynamic_slice_in_dim(packed, core * half, half, 0)
    piece = kept + lax.ppermute(sent, "wide", twins)
    piece = jnp.sum(over_grp(piece.reshape(groups, -1, LANES)), axis=0)
    piece = jnp.sum(over_wide(piece.reshape(wide // 2, -1, LANES)), axis=0)
    held = jnp.concatenate([piece, mean_rows], axis=0)
    held = spread(held, over_wide, wide // 2)
    held = spread(held, over_grp, groups)
    held = held.reshape((-1,) + held.shape[2:])
    other = lax.ppermute(held, "wide", twins)
    half = held.shape[0]
    return held, other, jnp.stack([core * half, (1 - core) * half])


def factor_block(block, upper_ref, inverse_ref):
    groups = LANES // SUB
    tiles = [block[SUB * p : SUB * (p + 1), :] for p in range(groups)]
    row_at = lax.broadcasted_iota(jnp.int32, (SUB, LANES), 0)
    lane_at = lax.broadcasted_iota(jnp.int32, (SUB, LANES), 1)
    unit = [
        jnp.where(lane_at == row_at + SUB * p, 1.0, 0.0).astype(jnp.float32)
        for p in range(groups)
    ]
    for g in range(groups):
        base = SUB * g
        ahead = g + 1 < groups
        rows = [over_rows(tiles[g], i) for i in range(SUB)]
        s = {
            (i, j): over_lanes(rows[i], base + j) for i in range(SUB) for j in range(i, SUB)
        }
        carried = [over_rows(unit[g], i) for i in range(SUB)]
        if ahead:
            column = [over_lanes(tiles[g + 1], base + i) for i in range(SUB)]
        scale = []
        for j in range(SUB):
            r = lax.rsqrt(s[j, j])
            scale.append(r)
            for k in range(j + 1, SUB):
                s[j, k] = s[j, k] * r
            for k in range(j + 1, SUB):
                for m in range(k, SUB):
                    s[k, m] = s[k, m] - s[j, k] * s[j, m]
            rows[j] = rows[j] * r
            carried[j] = carried[j] * r
            for k in range(j + 1, SUB):
                rows[k] = rows[k] - s[j, k] * rows[j]
                carried[k] = carried[k] - s[j, k] * carried[j]
            if ahead:
                column[j] = column[j] * r
                for k in range(j + 1, SUB):
                    column[k] = column[k] - column[j] * s[j, k]
                tiles[g + 1] = tiles[g + 1] - column[j] * rows[j]
                unit[g + 1] = unit[g + 1] - column[j] * carried[j]
            upper_ref[base + j : base + j + 1, :] = rows[j][:1, :]
            inverse_ref[base + j : base + j + 1, :] = carried[j][:1, :]
        if g + 2 < groups:
            for i in reversed(range(SUB)):
                for k in range(i + 1, SUB):
                    rows[i] = rows[i] - s[i, k] * rows[k]
                    carried[i] = carried[i] - s[i, k] * carried[k]
                rows[i] = rows[i] * scale[i]
                carried[i] = carried[i] * scale[i]
        for p in range(g + 2, groups):
            column = [over_lanes(tiles[p], base + i) for i in range(SUB)]
            tiles[p] = tiles[p] - tree_sum([c * x for c, x in zip(column, rows)])
            unit[p] = unit[p] - tree_sum([c * x for c, x in zip(column, carried)])
        yield


def tree_sum(terms):
    while len(terms) > 1:
        terms = [a + b for a, b in zip(terms[::2], terms[1::2])]
    return terms[0]


def in_three(values):
    high = values.astype(jnp.bfloat16)
    rest = values - high.astype(jnp.float32)
    middle = rest.astype(jnp.bfloat16)
    return high, middle, (rest - middle.astype(jnp.float32)).astype(jnp.bfloat16)


def left_parts(values):
    high, middle, low = in_three(values)
    return jnp.concatenate([high, middle], axis=1), jnp.concatenate([low, high], axis=1)


def right_parts(values):
    high, middle, low = in_three(values)
    stack = lambda a, b: jnp.concatenate([a, b], axis=0)
    return stack(high, high), stack(middle, middle), stack(high, low)


def parts_dot(left, right):
    plain = lambda a, b: fast_dot(a, b, ((1,), (0,)))
    return (plain(left[1], right[2]) + plain(left[0], right[1])) + plain(left[0], right[0])


def factor_kernel(
    x_hbm,
    held_ref,
    other_ref,
    numbers_ref,
    count_ref,
    out_hbm,
    factor_ref,
    work,
    packed,
    means_scr,
    upper_ref,
    inverse_ref,
    x_ref,
    x_high,
    x_low,
    high_ref,
    low_ref,
    out_ref,
    arrived,
    left_for_out,
):
    rows_in = chunk_copies(x_hbm, x_ref, arrived)
    for copy in rows_in:
        copy.start()
    half = held_ref.shape[0]
    pieces = 2 * half
    width = factor_ref.shape[0]
    blocks = width // LANES
    piece_rows = packed.shape[0] // pieces

    for part, ref in enumerate((held_ref, other_ref)):

        def unpack(q, _):
            p = numbers_ref[part] ^ q
            to = pl.multiple_of(p * piece_rows, SUB)
            packed[pl.ds(to, piece_rows), :] = ref[q, :piece_rows, :]
            to = pl.multiple_of(p * SUB, SUB)
            means_scr[pl.ds(to, SUB), :] = ref[q, piece_rows : piece_rows + SUB, :]
            return 0

        lax.fori_loop(0, half, unpack, 0, unroll=True)

    stacked = means_scr[...].reshape(pieces, SUB, LANES)
    middle = jnp.mean(stacked, axis=0)
    apart = stacked - middle[None]
    wide = jnp.concatenate([apart[:, b, :] for b in range(blocks)], axis=1)
    col_mean = jnp.concatenate([middle[b : b + 1, :] for b in range(blocks)], axis=1)
    total_scale = count_ref[1]
    place = {block: LANES * p for p, block in enumerate(upper_blocks(width))}
    span = lambda b, e=None: slice(LANES * b, LANES * (b + 1 if e is None else e))

    def gather(i, first, end):
        between = dot(wide[:, span(i)], wide[:, span(first, end)], ((0,), (0,)))
        for j in range(first, end):
            work[span(i), span(j)] = (
                packed[place[i, j] : place[i, j] + LANES, :]
                + between[:, span(j - first)] * count_ref[0]
            )

    def write_row(k):
        row_at = lax.broadcasted_iota(jnp.int32, (LANES, LANES), 0)
        col_at = lax.broadcasted_iota(jnp.int32, (LANES, LANES), 1)
        zero = jnp.zeros((LANES, LANES), jnp.float32)
        for j in range(blocks):
            if j < k:
                factor, back = zero, work[span(k), span(j)]
            elif j > k:
                factor, back = work[span(k), span(j)], zero
            else:
                factor = jnp.where(col_at >= row_at, upper_ref[k % 2], 0.0)
                back = inverse_ref[k % 2]
            factor_ref[span(k), span(j)] = factor * (1.0 / total_scale)
            high, low = split((back * total_scale).T)
            high_ref[span(j), span(k)] = high
            low_ref[span(j), span(k)] = low

    def centre(chunk):
        here = slice(TILE * chunk, TILE * (chunk + 1))
        rows_in[chunk].wait()
        high, low = split(x_ref[here, :] - col_mean)
        x_high[here, :] = high
        x_low[here, :] = low

    rows_out = []

    def whiten(chunk, right):
        here = slice(TILE * chunk, TILE * (chunk + 1))
        cols, deep = slice(right, right + TILE), slice(0, right + TILE)
        tile = fast_dot(x_low[here, deep], high_ref[deep, cols], ((1,), (0,)))
        tile = tile + fast_dot(x_high[here, deep], low_ref[deep, cols], ((1,), (0,)))
        out_ref[here, cols] = tile + fast_dot(
            x_high[here, deep], high_ref[deep, cols], ((1,), (0,))
        )
        copy = pltpu.make_async_copy(
            out_ref.at[here, cols], out_hbm.at[here, cols], left_for_out.at[len(rows_out)]
        )
        copy.start()
        rows_out.append(copy)

    def below(k, i, left, right, first):
        change = parts_dot(left, [r[:, : LANES * (k + 1)] for r in right])
        if k:
            work[span(i), span(0, k)] = work[span(i), span(0, k)] - change[:, : LANES * k]
        work[span(i), span(k)] = -change[:, LANES * k :]
        if first < blocks:
            cols = span(first, blocks)
            work[span(i), cols] = work[span(i), cols] - parts_dot(
                left, [r[:, cols] for r in right]
            )

    def later(k, left, solved, turned):
        row = {}

        def solve_rest():
            if k:
                cols = span(0, k)
                work[span(k), cols] = parts_dot(left, right_parts(work[span(k), cols]))
            if k + 2 < blocks:
                cols = span(k + 2, blocks)
                work[span(k), cols] = parts_dot(left, right_parts(work[span(k), cols]))
            if k + 1 < blocks:
                work[span(k), span(k + 1)] = solved
            row["parts"] = right_parts(
                jnp.concatenate(
                    [
                        inverse_ref[k % 2] if j == k else work[span(k), span(j)]
                        for j in range(blocks)
                    ],
                    axis=1,
                )
            )

        todo = [solve_rest]
        for i in range(k + 1, blocks):

            def one(i=i):
                lead = turned if i == k + 1 else left_parts(work[span(k), span(i)].T)
                below(k, i, lead, row["parts"], max(i, k + 2))

            todo.append(one)
        todo.append(lambda: write_row(k))
        return todo

    gather(0, 0, 1)
    todo = [lambda: gather(0, 1, blocks)]
    todo += [lambda i=i: gather(i, i, blocks) for i in range(1, blocks)]
    todo += [lambda c=c: centre(c) for c in range(len(rows_in))]
    waiting = []
    for k in range(blocks):
        groups = LANES // SUB
        done = 0
        steps = factor_block(work[span(k), span(k)], upper_ref.at[k % 2], inverse_ref.at[k % 2])
        for g, _ in enumerate(steps):
            due = -(-len(todo) * (g + 1) // groups)
            for piece in todo[done:due]:
                piece()
            done = due
        left = left_parts(inverse_ref[k % 2])
        solved = turned = None
        if k + 1 < blocks:
            solved = parts_dot(left, right_parts(work[span(k), span(k + 1)]))
            turned = left_parts(solved.T)
            work[span(k + 1), span(k + 1)] = work[span(k + 1), span(k + 1)] - parts_dot(
                turned, right_parts(solved)
            )
        todo = later(k, left, solved, turned) + waiting
        waiting = []
        if LANES * (k + 1) % TILE == 0:
            right = LANES * (k + 1) - TILE
            white = [lambda c=c, r=right: whiten(c, r) for c in range(len(rows_in))]
            share = len(white) if k + 1 == blocks else len(white) // 2
            todo, waiting = todo + white[:share], white[share:]
    for piece in todo:
        piece()
    for copy in rows_out:
        copy.wait()


def factor_and_whiten(embeddings, held, other, numbers, piece_rows):
    rows, width = embeddings.shape
    pieces = 2 * held.shape[0]
    vmem = pl.BlockSpec(memory_space=pltpu.VMEM)
    smem = pl.BlockSpec(memory_space=pltpu.SMEM)
    anywhere = pl.BlockSpec(memory_space=pl.ANY)
    chunks = rows // TILE
    counts = jnp.array([rows, (rows * pieces) ** 0.5], jnp.float32)
    return pl.pallas_call(
        factor_kernel,
        out_shape=(
            jax.ShapeDtypeStruct((rows, width), jnp.float32),
            jax.ShapeDtypeStruct((width, width), jnp.float32),
        ),
        in_specs=[anywhere, vmem, vmem, smem, smem],
        out_specs=(anywhere, vmem),
        scratch_shapes=[
            pltpu.VMEM((width, width), jnp.float32),
            pltpu.VMEM((pieces * piece_rows, LANES), jnp.float32),
            pltpu.VMEM((pieces * SUB, LANES), jnp.float32),
            pltpu.VMEM((2, LANES, LANES), jnp.float32),
            pltpu.VMEM((2, LANES, LANES), jnp.float32),
            pltpu.VMEM((rows, width), jnp.float32),
            pltpu.VMEM((rows, width), jnp.bfloat16),
            pltpu.VMEM((rows, width), jnp.bfloat16),
            pltpu.VMEM((width, width), jnp.bfloat16),
            pltpu.VMEM((width, width), jnp.bfloat16),
            pltpu.VMEM((rows, width), jnp.float32),
            pltpu.SemaphoreType.DMA((chunks,)),
            pltpu.SemaphoreType.DMA((chunks * (width // TILE),)),
        ],
        compiler_params=pltpu.CompilerParams(vmem_limit_bytes=48 * 2**20),
    )(embeddings, held, other, numbers, counts)


def shards(embeddings):
    _, width = embeddings.shape
    devices = lax.axis_size("grp") * lax.axis_size("wide")
    used = LANES * len(upper_blocks(width))
    piece_rows = -(-used // (SUB * devices)) * SUB
    packed, mean_rows = local_gram(embeddings, piece_rows * devices, SUB)
    held, other, numbers = sum_in_pieces(packed, mean_rows)
    return factor_and_whiten(embeddings, held, other, numbers, piece_rows)


def solution(mesh):
    rows = P(AXES, None)
    return jax.shard_map(
        shards,
        mesh=mesh,
        in_specs=(rows,),
        out_specs=(rows, P()),
        check_vma=False,
    )
```

```python
import jax
import jax.numpy as jnp
from jax import lax
from jax.experimental import pallas as pl
from jax.experimental.pallas import tpu as pltpu
from jax.sharding import PartitionSpec as P

AXES = ("grp", "wide")
LANES = 128
SUB = 8
TILE = 256
HIGHEST = lax.Precision.HIGHEST


def dot(a, b, dims):
    return lax.dot_general(
        a, b, (dims, ((), ())), precision=HIGHEST, preferred_element_type=jnp.float32
    )


def over_lanes(tile, lane):
    return jnp.broadcast_to(tile[:, lane : lane + 1], (SUB, LANES))


def over_rows(tile, row):
    return jnp.broadcast_to(tile[row : row + 1, :], (SUB, LANES))


def split(values):
    high = values.astype(jnp.bfloat16)
    return high, (values - high.astype(jnp.float32)).astype(jnp.bfloat16)


def fast_dot(a, b, dims):
    return lax.dot_general(a, b, (dims, ((), ())), preferred_element_type=jnp.float32)


def upper_blocks(width):
    n = width // LANES
    return [(i, j) for i in range(n) for j in range(i, n)]


def chunk_copies(source, target, arrived):
    return [
        pltpu.make_async_copy(
            source.at[pl.ds(r, TILE), :], target.at[pl.ds(r, TILE), :], arrived.at[r // TILE]
        )
        for r in range(0, source.shape[0], TILE)
    ]


def gram_kernel(x_hbm, packed_ref, mean_ref, x_ref, split_ref, arrived):
    rows, width = x_ref.shape
    copies = chunk_copies(x_hbm, x_ref, arrived)
    for copy in copies:
        copy.start()
    total = jnp.zeros((SUB, width), jnp.float32)
    for r in range(0, rows, LANES):
        if r % TILE == 0:
            copies[r // TILE].wait()
        part = x_ref[r : r + LANES, :]
        for q in range(0, LANES, SUB):
            total = total + part[q : q + SUB, :]
    mean = jnp.sum(total, axis=0, keepdims=True) * (1.0 / rows)
    for r in range(0, rows, LANES):
        high, low = split(x_ref[r : r + LANES, :] - mean)
        for part, value in enumerate((high, low, low, high)):
            split_ref[rows * part + r : rows * part + r + LANES, :] = value
    place = {block: LANES * p for p, block in enumerate(upper_blocks(width))}
    for left in range(0, width, TILE):
        turned = split_ref[: 2 * rows, left : left + TILE].T
        turned = jnp.concatenate([turned, turned], axis=1)
        for right in range(left, width, TILE):
            here = slice(right, right + TILE)
            tile = fast_dot(turned, split_ref[:, here], ((1,), (0,)))
            for a in range(0, TILE, LANES):
                for b in range(0, TILE, LANES):
                    block = ((left + a) // LANES, (right + b) // LANES)
                    if block in place:
                        packed_ref[place[block] : place[block] + LANES, :] = tile[
                            a : a + LANES, b : b + LANES
                        ]
    used = LANES * len(place)
    if packed_ref.shape[0] > used:
        packed_ref[used:, :] = jnp.zeros((packed_ref.shape[0] - used, LANES), jnp.float32)
    mean_ref[...] = jnp.zeros(mean_ref.shape, jnp.float32)
    for b in range(width // LANES):
        mean_ref[b : b + 1, :] = mean[:, LANES * b : LANES * (b + 1)]


def local_gram(embeddings, packed_rows, mean_rows):
    rows, width = embeddings.shape
    return pl.pallas_call(
        gram_kernel,
        out_shape=(
            jax.ShapeDtypeStruct((packed_rows, LANES), jnp.float32),
            jax.ShapeDtypeStruct((mean_rows, LANES), jnp.float32),
        ),
        in_specs=[pl.BlockSpec(memory_space=pl.ANY)],
        out_specs=(pl.BlockSpec(memory_space=pltpu.VMEM),) * 2,
        scratch_shapes=[pltpu.VMEM((rows, width), jnp.float32)]
        + [pltpu.VMEM((4 * rows, width), jnp.bfloat16)]
        + [pltpu.SemaphoreType.DMA((rows // TILE,))],
        compiler_params=pltpu.CompilerParams(vmem_limit_bytes=60 * 2**20),
    )(embeddings)


def sum_in_pieces(packed, mean_rows):
    groups, wide = lax.axis_size("grp"), lax.axis_size("wide")
    core = lax.axis_index("wide") & 1
    twins = [(d, d ^ 1) for d in range(wide)]
    same_core = [list(range(c, wide, 2)) for c in range(2)]

    def over_grp(parts):
        return lax.all_to_all(parts, "grp", 0, 0)

    def over_wide(parts):
        return lax.all_to_all(parts, "wide", 0, 0, axis_index_groups=same_core)

    def spread(parts, trade, count):
        return trade(jnp.broadcast_to(parts[None], (count,) + parts.shape))

    half = packed.shape[0] // 2
    sent = lax.dynamic_slice_in_dim(packed, (1 - core) * half, half, 0)
    kept = lax.dynamic_slice_in_dim(packed, core * half, half, 0)
    piece = kept + lax.ppermute(sent, "wide", twins)
    piece = jnp.sum(over_grp(piece.reshape(groups, -1, LANES)), axis=0)
    piece = jnp.sum(over_wide(piece.reshape(wide // 2, -1, LANES)), axis=0)
    held = jnp.concatenate([piece, mean_rows], axis=0)
    held = spread(held, over_wide, wide // 2)
    held = spread(held, over_grp, groups)
    held = held.reshape((-1,) + held.shape[2:])
    other = lax.ppermute(held, "wide", twins)
    half = held.shape[0]
    return held, other, jnp.stack([core * half, (1 - core) * half])


def factor_block(block, upper_ref, inverse_ref):
    groups = LANES // SUB
    tiles = [block[SUB * p : SUB * (p + 1), :] for p in range(groups)]
    lane_at = lax.broadcasted_iota(jnp.int32, (SUB, LANES), 1)
    for g in range(groups):
        base = SUB * g
        ahead = g + 1 < groups
        own = (lane_at >= base) & (lane_at < base + SUB)
        at_lane = [lane_at == base + i for i in range(SUB)]
        rows = [over_rows(tiles[g], i) for i in range(SUB)]
        s = {
            (i, j): over_lanes(rows[i], base + j) for i in range(SUB) for j in range(i, SUB)
        }
        rows = [
            jnp.where(own, jnp.where(at_lane[i], 1.0, 0.0), rows[i]) for i in range(SUB)
        ]
        if ahead:
            column = [over_lanes(tiles[g + 1], base + i) for i in range(SUB)]
            tiles[g + 1] = jnp.where(own, 0.0, tiles[g + 1])
        scale = []
        for j in range(SUB):
            r = lax.rsqrt(s[j, j])
            scale.append(r)
            for k in range(j, SUB):
                s[j, k] = s[j, k] * r
            for k in range(j + 1, SUB):
                for m in range(k, SUB):
                    s[k, m] = s[k, m] - s[j, k] * s[j, m]
            rows[j] = rows[j] * r
            for k in range(j + 1, SUB):
                rows[k] = rows[k] - s[j, k] * rows[j]
            if ahead:
                column[j] = column[j] * r
                for k in range(j + 1, SUB):
                    column[k] = column[k] - column[j] * s[j, k]
                tiles[g + 1] = tiles[g + 1] - column[j] * rows[j]
            inverse_ref[base + j : base + j + 1, :] = rows[j][:1, :]
            upper = rows[j]
            for k in range(j, SUB):
                upper = jnp.where(at_lane[k], s[j, k], upper)
            upper_ref[base + j : base + j + 1, :] = upper[:1, :]
        if g + 2 < groups:
            for i in reversed(range(SUB)):
                for k in range(i + 1, SUB):
                    rows[i] = rows[i] - s[i, k] * rows[k]
                rows[i] = rows[i] * scale[i]
        for p in range(g + 2, groups):
            column = [over_lanes(tiles[p], base + i) for i in range(SUB)]
            change = tree_sum([c * x for c, x in zip(column, rows)])
            tiles[p] = jnp.where(own, 0.0, tiles[p]) - change
        yield
    row_group = lax.broadcasted_iota(jnp.int32, (LANES, LANES), 0) // SUB
    lane_group = lax.broadcasted_iota(jnp.int32, (LANES, LANES), 1) // SUB
    inverse_ref[...] = jnp.where(lane_group <= row_group, inverse_ref[...], 0.0)


def tree_sum(terms):
    while len(terms) > 1:
        terms = [a + b for a, b in zip(terms[::2], terms[1::2])]
    return terms[0]


def in_three(values):
    high = values.astype(jnp.bfloat16)
    rest = values - high.astype(jnp.float32)
    middle = rest.astype(jnp.bfloat16)
    return high, middle, (rest - middle.astype(jnp.float32)).astype(jnp.bfloat16)


def left_parts(values):
    high, middle, low = in_three(values)
    return jnp.concatenate([high, middle, high, middle, high, low], axis=1)


def right_parts(values):
    high, middle, low = in_three(values)
    return jnp.concatenate([high, high, middle, middle, low, high], axis=0)


def parts_dot(left, right):
    return fast_dot(left, right, ((1,), (0,)))


def factor_kernel(
    x_hbm,
    held_ref,
    other_ref,
    numbers_ref,
    count_ref,
    out_hbm,
    factor_ref,
    work,
    packed,
    means_scr,
    upper_ref,
    inverse_ref,
    x_ref,
    x_high,
    x_low,
    high_ref,
    low_ref,
    out_ref,
    arrived,
    left_for_out,
):
    rows_in = chunk_copies(x_hbm, x_ref, arrived)
    for copy in rows_in:
        copy.start()
    half = held_ref.shape[0]
    pieces = 2 * half
    width = factor_ref.shape[0]
    blocks = width // LANES
    piece_rows = packed.shape[0] // pieces

    for part, ref in enumerate((held_ref, other_ref)):

        def unpack(q, _):
            p = numbers_ref[part] ^ q
            to = pl.multiple_of(p * piece_rows, SUB)
            packed[pl.ds(to, piece_rows), :] = ref[q, :piece_rows, :]
            to = pl.multiple_of(p * SUB, SUB)
            means_scr[pl.ds(to, SUB), :] = ref[q, piece_rows : piece_rows + SUB, :]
            return 0

        lax.fori_loop(0, half, unpack, 0, unroll=True)

    stacked = means_scr[...].reshape(pieces, SUB, LANES)
    middle = jnp.mean(stacked, axis=0)
    apart = stacked - middle[None]
    wide = jnp.concatenate([apart[:, b, :] for b in range(blocks)], axis=1)
    col_mean = jnp.concatenate([middle[b : b + 1, :] for b in range(blocks)], axis=1)
    total_scale = count_ref[1]
    place = {block: LANES * p for p, block in enumerate(upper_blocks(width))}
    span = lambda b, e=None: slice(LANES * b, LANES * (b + 1 if e is None else e))

    def gather(i, first, end):
        between = dot(wide[:, span(i)], wide[:, span(first, end)], ((0,), (0,)))
        for j in range(first, end):
            work[span(i), span(j)] = (
                packed[place[i, j] : place[i, j] + LANES, :]
                + between[:, span(j - first)] * count_ref[0]
            )

    def write_row(k):
        row_at = lax.broadcasted_iota(jnp.int32, (LANES, LANES), 0)
        col_at = lax.broadcasted_iota(jnp.int32, (LANES, LANES), 1)
        zero = jnp.zeros((LANES, LANES), jnp.float32)
        for j in range(blocks):
            if j < k:
                factor, back = zero, work[span(k), span(j)]
            elif j > k:
                factor, back = work[span(k), span(j)], zero
            else:
                factor = jnp.where(col_at >= row_at, upper_ref[k % 2], 0.0)
                back = inverse_ref[k % 2]
            factor_ref[span(k), span(j)] = factor * (1.0 / total_scale)
            high, low = split((back * total_scale).T)
            high_ref[span(j), span(k)] = high
            low_ref[span(j), span(k)] = low

    def centre(chunk):
        here = slice(TILE * chunk, TILE * (chunk + 1))
        high, low = split(x_ref[here, :] - col_mean)
        x_high[here, :] = high
        x_low[here, :] = low

    rows_out = []
    whitened = []

    def whiten(chunk, right):
        here = slice(TILE * chunk, TILE * (chunk + 1))
        cols, deep = slice(right, right + TILE), slice(0, right + TILE)
        high, low = x_high[here, deep], x_low[here, deep]
        back_high, back_low = high_ref[deep, cols], low_ref[deep, cols]
        out_ref[here, cols] = fast_dot(
            jnp.concatenate([high, high, low], axis=1),
            jnp.concatenate([back_high, back_low, back_high], axis=0),
            ((1,), (0,)),
        )
        whitened.append((here, cols))

    def send_whitened():
        for here, cols in whitened[len(rows_out) :]:
            copy = pltpu.make_async_copy(
                out_ref.at[here, cols], out_hbm.at[here, cols], left_for_out.at[len(rows_out)]
            )
            copy.start()
            rows_out.append(copy)

    def below(k, i, left, right, first):
        change = parts_dot(left, right[:, : LANES * (k + 1)])
        if k:
            work[span(i), span(0, k)] = work[span(i), span(0, k)] - change[:, : LANES * k]
        work[span(i), span(k)] = -change[:, LANES * k :]
        if first < blocks:
            cols = span(first, blocks)
            work[span(i), cols] = work[span(i), cols] - parts_dot(left, right[:, cols])

    def later(k, left, solved, turned):
        row = {}

        def solve_rest():
            if k:
                cols = span(0, k)
                work[span(k), cols] = parts_dot(left, right_parts(work[span(k), cols]))
            if k + 2 < blocks:
                cols = span(k + 2, blocks)
                work[span(k), cols] = parts_dot(left, right_parts(work[span(k), cols]))
            if k + 1 < blocks:
                work[span(k), span(k + 1)] = solved
            row["parts"] = right_parts(
                jnp.concatenate(
                    [
                        inverse_ref[k % 2] if j == k else work[span(k), span(j)]
                        for j in range(blocks)
                    ],
                    axis=1,
                )
            )

        todo = [solve_rest]
        for i in range(k + 1, blocks):

            def one(i=i):
                lead = turned if i == k + 1 else left_parts(work[span(k), span(i)].T)
                below(k, i, lead, row["parts"], max(i, k + 2))

            todo.append(one)
        todo.append(lambda: write_row(k))
        return todo

    gather(0, 0, 1)
    todo = [lambda: gather(0, 1, blocks)]
    todo += [lambda i=i: gather(i, i, blocks) for i in range(1, blocks)]
    waiting = []
    for k in range(blocks):
        groups = LANES // SUB
        done = 0
        if k == 1:
            for copy in rows_in:
                copy.wait()
            todo += [lambda c=c: centre(c) for c in range(len(rows_in))]
        steps = factor_block(work[span(k), span(k)], upper_ref.at[k % 2], inverse_ref.at[k % 2])
        for g, _ in enumerate(steps):
            due = -(-len(todo) * (g + 1) // groups)
            for piece in todo[done:due]:
                piece()
            done = due
        send_whitened()
        left = left_parts(inverse_ref[k % 2])
        solved = turned = None
        if k + 1 < blocks:
            solved = parts_dot(left, right_parts(work[span(k), span(k + 1)]))
            turned = left_parts(solved.T)
            work[span(k + 1), span(k + 1)] = work[span(k + 1), span(k + 1)] - parts_dot(
                turned, right_parts(solved)
            )
        todo = later(k, left, solved, turned) + waiting
        waiting = []
        if LANES * (k + 1) % TILE == 0:
            right = LANES * (k + 1) - TILE
            white = [lambda c=c, r=right: whiten(c, r) for c in range(len(rows_in))]
            share = len(white) if k + 1 == blocks else len(white) // 2
            todo, waiting = todo + white[:share], white[share:]
    for piece in todo:
        piece()
        send_whitened()
    for copy in rows_out:
        copy.wait()


def factor_and_whiten(embeddings, held, other, numbers, piece_rows):
    rows, width = embeddings.shape
    pieces = 2 * held.shape[0]
    vmem = pl.BlockSpec(memory_space=pltpu.VMEM)
    smem = pl.BlockSpec(memory_space=pltpu.SMEM)
    anywhere = pl.BlockSpec(memory_space=pl.ANY)
    chunks = rows // TILE
    counts = jnp.array([rows, (rows * pieces) ** 0.5], jnp.float32)
    return pl.pallas_call(
        factor_kernel,
        out_shape=(
            jax.ShapeDtypeStruct((rows, width), jnp.float32),
            jax.ShapeDtypeStruct((width, width), jnp.float32),
        ),
        in_specs=[anywhere, vmem, vmem, smem, smem],
        out_specs=(anywhere, vmem),
        scratch_shapes=[
            pltpu.VMEM((width, width), jnp.float32),
            pltpu.VMEM((pieces * piece_rows, LANES), jnp.float32),
            pltpu.VMEM((pieces * SUB, LANES), jnp.float32),
            pltpu.VMEM((2, LANES, LANES), jnp.float32),
            pltpu.VMEM((2, LANES, LANES), jnp.float32),
            pltpu.VMEM((rows, width), jnp.float32),
            pltpu.VMEM((rows, width), jnp.bfloat16),
            pltpu.VMEM((rows, width), jnp.bfloat16),
            pltpu.VMEM((width, width), jnp.bfloat16),
            pltpu.VMEM((width, width), jnp.bfloat16),
            pltpu.VMEM((rows, width), jnp.float32),
            pltpu.SemaphoreType.DMA((chunks,)),
            pltpu.SemaphoreType.DMA((chunks * (width // TILE),)),
        ],
        compiler_params=pltpu.CompilerParams(vmem_limit_bytes=48 * 2**20),
    )(embeddings, held, other, numbers, counts)


def shards(embeddings):
    _, width = embeddings.shape
    devices = lax.axis_size("grp") * lax.axis_size("wide")
    used = LANES * len(upper_blocks(width))
    piece_rows = -(-used // (SUB * devices)) * SUB
    packed, mean_rows = local_gram(embeddings, piece_rows * devices, SUB)
    held, other, numbers = sum_in_pieces(packed, mean_rows)
    return factor_and_whiten(embeddings, held, other, numbers, piece_rows)


def solution(mesh):
    rows = P(AXES, None)
    return jax.shard_map(
        shards,
        mesh=mesh,
        in_specs=(rows,),
        out_specs=(rows, P()),
        check_vma=False,
    )
```

```python
import jax
import jax.numpy as jnp
from jax import lax
from jax.experimental import pallas as pl
from jax.experimental.pallas import tpu as pltpu
from jax.sharding import PartitionSpec as P

AXES = ("grp", "wide")
LANES = 128
SUB = 8
TILE = 256
HIGHEST = lax.Precision.HIGHEST


def dot(a, b, dims):
    return lax.dot_general(
        a, b, (dims, ((), ())), precision=HIGHEST, preferred_element_type=jnp.float32
    )


def over_lanes(tile, lane):
    return jnp.broadcast_to(tile[:, lane : lane + 1], (SUB, LANES))


def over_rows(tile, row):
    return jnp.broadcast_to(tile[row : row + 1, :], (SUB, LANES))


def split(values):
    high = values.astype(jnp.bfloat16)
    return high, (values - high.astype(jnp.float32)).astype(jnp.bfloat16)


def fast_dot(a, b, dims):
    return lax.dot_general(a, b, (dims, ((), ())), preferred_element_type=jnp.float32)


def upper_blocks(width):
    n = width // LANES
    return [(i, j) for i in range(n) for j in range(i, n)]


def chunk_copies(source, target, arrived):
    return [
        pltpu.make_async_copy(
            source.at[pl.ds(r, TILE), :], target.at[pl.ds(r, TILE), :], arrived.at[r // TILE]
        )
        for r in range(0, source.shape[0], TILE)
    ]


def gram_kernel(x_ref, packed_ref, mean_ref, both_ref, swapped_ref):
    rows, width = x_ref.shape
    total = jnp.zeros((SUB, width), jnp.float32)
    for r in range(0, rows, LANES):
        part = x_ref[r : r + LANES, :]
        for q in range(0, LANES, SUB):
            total = total + part[q : q + SUB, :]
    mean = jnp.sum(total, axis=0, keepdims=True) * (1.0 / rows)
    for r in range(0, rows, LANES):
        high, low = split(x_ref[r : r + LANES, :] - mean)
        both_ref[r : r + LANES, :] = high
        both_ref[rows + r : rows + r + LANES, :] = low
        swapped_ref[r : r + LANES, :] = low
        swapped_ref[rows + r : rows + r + LANES, :] = high
    place = {block: LANES * p for p, block in enumerate(upper_blocks(width))}
    for left in range(0, width, TILE):
        turned = both_ref[:, left : left + TILE].T
        for right in range(left, width, TILE):
            here = slice(right, right + TILE)
            tile = fast_dot(turned, both_ref[:, here], ((1,), (0,)))
            tile = tile + fast_dot(turned, swapped_ref[:, here], ((1,), (0,)))
            for a in range(0, TILE, LANES):
                for b in range(0, TILE, LANES):
                    block = ((left + a) // LANES, (right + b) // LANES)
                    if block in place:
                        packed_ref[place[block] : place[block] + LANES, :] = tile[
                            a : a + LANES, b : b + LANES
                        ]
    used = LANES * len(place)
    if packed_ref.shape[0] > used:
        packed_ref[used:, :] = jnp.zeros((packed_ref.shape[0] - used, LANES), jnp.float32)
    mean_ref[...] = jnp.zeros(mean_ref.shape, jnp.float32)
    for b in range(width // LANES):
        mean_ref[b : b + 1, :] = mean[:, LANES * b : LANES * (b + 1)]


def local_gram(embeddings, packed_rows, mean_rows):
    rows, width = embeddings.shape
    return pl.pallas_call(
        gram_kernel,
        out_shape=(
            jax.ShapeDtypeStruct((packed_rows, LANES), jnp.float32),
            jax.ShapeDtypeStruct((mean_rows, LANES), jnp.float32),
        ),
        in_specs=[pl.BlockSpec(memory_space=pltpu.VMEM)],
        out_specs=(pl.BlockSpec(memory_space=pltpu.VMEM),) * 2,
        scratch_shapes=[pltpu.VMEM((2 * rows, width), jnp.bfloat16)] * 2,
        compiler_params=pltpu.CompilerParams(vmem_limit_bytes=48 * 2**20),
    )(embeddings)


def sum_in_pieces(packed, mean_rows):
    groups, wide = lax.axis_size("grp"), lax.axis_size("wide")
    core = lax.axis_index("wide") & 1
    twins = [(d, d ^ 1) for d in range(wide)]
    same_core = [list(range(c, wide, 2)) for c in range(2)]

    def over_grp(parts):
        return lax.all_to_all(parts, "grp", 0, 0)

    def over_wide(parts):
        return lax.all_to_all(parts, "wide", 0, 0, axis_index_groups=same_core)

    def spread(parts, trade, count):
        return trade(jnp.broadcast_to(parts[None], (count,) + parts.shape))

    half = packed.shape[0] // 2
    sent = lax.dynamic_slice_in_dim(packed, (1 - core) * half, half, 0)
    kept = lax.dynamic_slice_in_dim(packed, core * half, half, 0)
    piece = kept + lax.ppermute(sent, "wide", twins)
    piece = jnp.sum(over_grp(piece.reshape(groups, -1, LANES)), axis=0)
    piece = jnp.sum(over_wide(piece.reshape(wide // 2, -1, LANES)), axis=0)
    held = jnp.concatenate([piece, mean_rows], axis=0)
    held = spread(held, over_wide, wide // 2)
    held = spread(held, over_grp, groups)
    held = held.reshape((-1,) + held.shape[2:])
    other = lax.ppermute(held, "wide", twins)
    half = held.shape[0]
    return held, other, jnp.stack([core * half, (1 - core) * half])


def factor_block(block, upper_ref, inverse_ref):
    groups = LANES // SUB
    tiles = [block[SUB * p : SUB * (p + 1), :] for p in range(groups)]
    lane_at = lax.broadcasted_iota(jnp.int32, (SUB, LANES), 1)
    for g in range(groups):
        base = SUB * g
        ahead = g + 1 < groups
        own = (lane_at >= base) & (lane_at < base + SUB)
        at_lane = [lane_at == base + i for i in range(SUB)]
        rows = [over_rows(tiles[g], i) for i in range(SUB)]
        s = {
            (i, j): over_lanes(rows[i], base + j) for i in range(SUB) for j in range(i, SUB)
        }
        rows = [
            jnp.where(own, jnp.where(at_lane[i], 1.0, 0.0), rows[i]) for i in range(SUB)
        ]
        if ahead:
            column = [over_lanes(tiles[g + 1], base + i) for i in range(SUB)]
            tiles[g + 1] = jnp.where(own, 0.0, tiles[g + 1])
        scale = []
        for j in range(SUB):
            r = lax.rsqrt(s[j, j])
            scale.append(r)
            for k in range(j, SUB):
                s[j, k] = s[j, k] * r
            for k in range(j + 1, SUB):
                for m in range(k, SUB):
                    s[k, m] = s[k, m] - s[j, k] * s[j, m]
            rows[j] = rows[j] * r
            for k in range(j + 1, SUB):
                rows[k] = rows[k] - s[j, k] * rows[j]
            if ahead:
                column[j] = column[j] * r
                for k in range(j + 1, SUB):
                    column[k] = column[k] - column[j] * s[j, k]
                tiles[g + 1] = tiles[g + 1] - column[j] * rows[j]
            inverse_ref[base + j : base + j + 1, :] = rows[j][:1, :]
            upper = rows[j]
            for k in range(j, SUB):
                upper = jnp.where(at_lane[k], s[j, k], upper)
            upper_ref[base + j : base + j + 1, :] = upper[:1, :]
        if g + 2 < groups:
            for i in reversed(range(SUB)):
                for k in range(i + 1, SUB):
                    rows[i] = rows[i] - s[i, k] * rows[k]
                rows[i] = rows[i] * scale[i]
        for p in range(g + 2, groups):
            column = [over_lanes(tiles[p], base + i) for i in range(SUB)]
            change = tree_sum([c * x for c, x in zip(column, rows)])
            tiles[p] = jnp.where(own, 0.0, tiles[p]) - change
        yield
    row_group = lax.broadcasted_iota(jnp.int32, (LANES, LANES), 0) // SUB
    lane_group = lax.broadcasted_iota(jnp.int32, (LANES, LANES), 1) // SUB
    inverse_ref[...] = jnp.where(lane_group <= row_group, inverse_ref[...], 0.0)


def tree_sum(terms):
    while len(terms) > 1:
        terms = [a + b for a, b in zip(terms[::2], terms[1::2])]
    return terms[0]


def in_three(values):
    high = values.astype(jnp.bfloat16)
    rest = values - high.astype(jnp.float32)
    middle = rest.astype(jnp.bfloat16)
    return high, middle, (rest - middle.astype(jnp.float32)).astype(jnp.bfloat16)


def left_parts(values):
    high, middle, low = in_three(values)
    return jnp.concatenate([high, middle], axis=1), jnp.concatenate([low, high], axis=1)


def right_parts(values):
    high, middle, low = in_three(values)
    stack = lambda a, b: jnp.concatenate([a, b], axis=0)
    return stack(high, high), stack(middle, middle), stack(high, low)


def parts_dot(left, right):
    plain = lambda a, b: fast_dot(a, b, ((1,), (0,)))
    return (plain(left[1], right[2]) + plain(left[0], right[1])) + plain(left[0], right[0])


def factor_kernel(
    x_hbm,
    held_ref,
    other_ref,
    numbers_ref,
    count_ref,
    out_hbm,
    factor_ref,
    work,
    packed,
    means_scr,
    upper_ref,
    inverse_ref,
    x_ref,
    x_high,
    x_low,
    high_ref,
    low_ref,
    out_ref,
    arrived,
    left_for_out,
):
    rows_in = chunk_copies(x_hbm, x_ref, arrived)
    for copy in rows_in:
        copy.start()
    half = held_ref.shape[0]
    pieces = 2 * half
    width = factor_ref.shape[0]
    blocks = width // LANES
    piece_rows = packed.shape[0] // pieces

    for part, ref in enumerate((held_ref, other_ref)):

        def unpack(q, _):
            p = numbers_ref[part] ^ q
            to = pl.multiple_of(p * piece_rows, SUB)
            packed[pl.ds(to, piece_rows), :] = ref[q, :piece_rows, :]
            to = pl.multiple_of(p * SUB, SUB)
            means_scr[pl.ds(to, SUB), :] = ref[q, piece_rows : piece_rows + SUB, :]
            return 0

        lax.fori_loop(0, half, unpack, 0, unroll=True)

    stacked = means_scr[...].reshape(pieces, SUB, LANES)
    middle = jnp.mean(stacked, axis=0)
    apart = stacked - middle[None]
    wide = jnp.concatenate([apart[:, b, :] for b in range(blocks)], axis=1)
    col_mean = jnp.concatenate([middle[b : b + 1, :] for b in range(blocks)], axis=1)
    total_scale = count_ref[1]
    place = {block: LANES * p for p, block in enumerate(upper_blocks(width))}
    span = lambda b, e=None: slice(LANES * b, LANES * (b + 1 if e is None else e))

    def gather(i, first, end):
        between = dot(wide[:, span(i)], wide[:, span(first, end)], ((0,), (0,)))
        for j in range(first, end):
            work[span(i), span(j)] = (
                packed[place[i, j] : place[i, j] + LANES, :]
                + between[:, span(j - first)] * count_ref[0]
            )

    def write_row(k):
        row_at = lax.broadcasted_iota(jnp.int32, (LANES, LANES), 0)
        col_at = lax.broadcasted_iota(jnp.int32, (LANES, LANES), 1)
        zero = jnp.zeros((LANES, LANES), jnp.float32)
        for j in range(blocks):
            if j < k:
                factor, back = zero, work[span(k), span(j)]
            elif j > k:
                factor, back = work[span(k), span(j)], zero
            else:
                factor = jnp.where(col_at >= row_at, upper_ref[k % 2], 0.0)
                back = inverse_ref[k % 2]
            factor_ref[span(k), span(j)] = factor * (1.0 / total_scale)
            high, low = split((back * total_scale).T)
            high_ref[span(j), span(k)] = high
            low_ref[span(j), span(k)] = low

    def centre(chunk):
        here = slice(TILE * chunk, TILE * (chunk + 1))
        rows_in[chunk].wait()
        high, low = split(x_ref[here, :] - col_mean)
        x_high[here, :] = high
        x_low[here, :] = low

    rows_out = []

    def whiten(chunk, right):
        here = slice(TILE * chunk, TILE * (chunk + 1))
        cols, deep = slice(right, right + TILE), slice(0, right + TILE)
        tile = fast_dot(x_low[here, deep], high_ref[deep, cols], ((1,), (0,)))
        tile = tile + fast_dot(x_high[here, deep], low_ref[deep, cols], ((1,), (0,)))
        out_ref[here, cols] = tile + fast_dot(
            x_high[here, deep], high_ref[deep, cols], ((1,), (0,))
        )
        copy = pltpu.make_async_copy(
            out_ref.at[here, cols], out_hbm.at[here, cols], left_for_out.at[len(rows_out)]
        )
        copy.start()
        rows_out.append(copy)

    def below(k, i, left, right, first):
        change = parts_dot(left, [r[:, : LANES * (k + 1)] for r in right])
        if k:
            work[span(i), span(0, k)] = work[span(i), span(0, k)] - change[:, : LANES * k]
        work[span(i), span(k)] = -change[:, LANES * k :]
        if first < blocks:
            cols = span(first, blocks)
            work[span(i), cols] = work[span(i), cols] - parts_dot(
                left, [r[:, cols] for r in right]
            )

    def later(k, left, solved, turned):
        row = {}

        def solve_rest():
            if k:
                cols = span(0, k)
                work[span(k), cols] = parts_dot(left, right_parts(work[span(k), cols]))
            if k + 2 < blocks:
                cols = span(k + 2, blocks)
                work[span(k), cols] = parts_dot(left, right_parts(work[span(k), cols]))
            if k + 1 < blocks:
                work[span(k), span(k + 1)] = solved
            row["parts"] = right_parts(
                jnp.concatenate(
                    [
                        inverse_ref[k % 2] if j == k else work[span(k), span(j)]
                        for j in range(blocks)
                    ],
                    axis=1,
                )
            )

        todo = [solve_rest]
        for i in range(k + 1, blocks):

            def one(i=i):
                lead = turned if i == k + 1 else left_parts(work[span(k), span(i)].T)
                below(k, i, lead, row["parts"], max(i, k + 2))

            todo.append(one)
        todo.append(lambda: write_row(k))
        return todo

    gather(0, 0, 1)
    todo = [lambda: gather(0, 1, blocks)]
    todo += [lambda i=i: gather(i, i, blocks) for i in range(1, blocks)]
    todo += [lambda c=c: centre(c) for c in range(len(rows_in))]
    waiting = []
    for k in range(blocks):
        groups = LANES // SUB
        done = 0
        steps = factor_block(work[span(k), span(k)], upper_ref.at[k % 2], inverse_ref.at[k % 2])
        for g, _ in enumerate(steps):
            due = -(-len(todo) * (g + 1) // groups)
            for piece in todo[done:due]:
                piece()
            done = due
        left = left_parts(inverse_ref[k % 2])
        solved = turned = None
        if k + 1 < blocks:
            solved = parts_dot(left, right_parts(work[span(k), span(k + 1)]))
            turned = left_parts(solved.T)
            work[span(k + 1), span(k + 1)] = work[span(k + 1), span(k + 1)] - parts_dot(
                turned, right_parts(solved)
            )
        todo = later(k, left, solved, turned) + waiting
        waiting = []
        if LANES * (k + 1) % TILE == 0:
            right = LANES * (k + 1) - TILE
            white = [lambda c=c, r=right: whiten(c, r) for c in range(len(rows_in))]
            share = len(white) if k + 1 == blocks else len(white) // 2
            todo, waiting = todo + white[:share], white[share:]
    for piece in todo:
        piece()
    for copy in rows_out:
        copy.wait()


def factor_and_whiten(embeddings, held, other, numbers, piece_rows):
    rows, width = embeddings.shape
    pieces = 2 * held.shape[0]
    vmem = pl.BlockSpec(memory_space=pltpu.VMEM)
    smem = pl.BlockSpec(memory_space=pltpu.SMEM)
    anywhere = pl.BlockSpec(memory_space=pl.ANY)
    chunks = rows // TILE
    counts = jnp.array([rows, (rows * pieces) ** 0.5], jnp.float32)
    return pl.pallas_call(
        factor_kernel,
        out_shape=(
            jax.ShapeDtypeStruct((rows, width), jnp.float32),
            jax.ShapeDtypeStruct((width, width), jnp.float32),
        ),
        in_specs=[anywhere, vmem, vmem, smem, smem],
        out_specs=(anywhere, vmem),
        scratch_shapes=[
            pltpu.VMEM((width, width), jnp.float32),
            pltpu.VMEM((pieces * piece_rows, LANES), jnp.float32),
            pltpu.VMEM((pieces * SUB, LANES), jnp.float32),
            pltpu.VMEM((2, LANES, LANES), jnp.float32),
            pltpu.VMEM((2, LANES, LANES), jnp.float32),
            pltpu.VMEM((rows, width), jnp.float32),
            pltpu.VMEM((rows, width), jnp.bfloat16),
            pltpu.VMEM((rows, width), jnp.bfloat16),
            pltpu.VMEM((width, width), jnp.bfloat16),
            pltpu.VMEM((width, width), jnp.bfloat16),
            pltpu.VMEM((rows, width), jnp.float32),
            pltpu.SemaphoreType.DMA((chunks,)),
            pltpu.SemaphoreType.DMA((chunks * (width // TILE),)),
        ],
        compiler_params=pltpu.CompilerParams(vmem_limit_bytes=48 * 2**20),
    )(embeddings, held, other, numbers, counts)


def shards(embeddings):
    _, width = embeddings.shape
    devices = lax.axis_size("grp") * lax.axis_size("wide")
    used = LANES * len(upper_blocks(width))
    piece_rows = -(-used // (SUB * devices)) * SUB
    packed, mean_rows = local_gram(embeddings, piece_rows * devices, SUB)
    held, other, numbers = sum_in_pieces(packed, mean_rows)
    return factor_and_whiten(embeddings, held, other, numbers, piece_rows)


def solution(mesh):
    rows = P(AXES, None)
    return jax.shard_map(
        shards,
        mesh=mesh,
        in_specs=(rows,),
        out_specs=(rows, P()),
        check_vma=False,
    )
```

```python
import jax
import jax.numpy as jnp
from jax import lax
from jax.experimental import pallas as pl
from jax.experimental.pallas import tpu as pltpu
from jax.sharding import PartitionSpec as P

AXES = ("grp", "wide")
LANES = 128
SUB = 8
TILE = 256
HIGHEST = lax.Precision.HIGHEST


def dot(a, b, dims):
    return lax.dot_general(
        a, b, (dims, ((), ())), precision=HIGHEST, preferred_element_type=jnp.float32
    )


def over_lanes(tile, lane):
    return jnp.broadcast_to(tile[:, lane : lane + 1], (SUB, LANES))


def over_rows(tile, row):
    return jnp.broadcast_to(tile[row : row + 1, :], (SUB, LANES))


def split(values):
    high = values.astype(jnp.bfloat16)
    return high, (values - high.astype(jnp.float32)).astype(jnp.bfloat16)


def fast_dot(a, b, dims):
    return lax.dot_general(a, b, (dims, ((), ())), preferred_element_type=jnp.float32)


def upper_blocks(width):
    n = width // LANES
    return [(i, j) for i in range(n) for j in range(i, n)]


def gram_kernel(x_ref, packed_ref, mean_ref, both_ref, swapped_ref):
    rows, width = x_ref.shape
    total = jnp.zeros((SUB, width), jnp.float32)
    for r in range(0, rows, LANES):
        part = x_ref[r : r + LANES, :]
        for q in range(0, LANES, SUB):
            total = total + part[q : q + SUB, :]
    mean = jnp.sum(total, axis=0, keepdims=True) * (1.0 / rows)
    for r in range(0, rows, LANES):
        high, low = split(x_ref[r : r + LANES, :] - mean)
        both_ref[r : r + LANES, :] = high
        both_ref[rows + r : rows + r + LANES, :] = low
        swapped_ref[r : r + LANES, :] = low
        swapped_ref[rows + r : rows + r + LANES, :] = high
    place = {block: LANES * p for p, block in enumerate(upper_blocks(width))}
    for left in range(0, width, TILE):
        turned = both_ref[:, left : left + TILE].T
        for right in range(left, width, TILE):
            here = slice(right, right + TILE)
            tile = fast_dot(turned, both_ref[:, here], ((1,), (0,)))
            tile = tile + fast_dot(turned, swapped_ref[:, here], ((1,), (0,)))
            for a in range(0, TILE, LANES):
                for b in range(0, TILE, LANES):
                    block = ((left + a) // LANES, (right + b) // LANES)
                    if block in place:
                        packed_ref[place[block] : place[block] + LANES, :] = tile[
                            a : a + LANES, b : b + LANES
                        ]
    used = LANES * len(place)
    if packed_ref.shape[0] > used:
        packed_ref[used:, :] = jnp.zeros((packed_ref.shape[0] - used, LANES), jnp.float32)
    mean_ref[...] = jnp.zeros(mean_ref.shape, jnp.float32)
    for b in range(width // LANES):
        mean_ref[b : b + 1, :] = mean[:, LANES * b : LANES * (b + 1)]


def local_gram(embeddings, packed_rows, mean_rows):
    rows, width = embeddings.shape
    return pl.pallas_call(
        gram_kernel,
        out_shape=(
            jax.ShapeDtypeStruct((packed_rows, LANES), jnp.float32),
            jax.ShapeDtypeStruct((mean_rows, LANES), jnp.float32),
        ),
        in_specs=[pl.BlockSpec(memory_space=pltpu.VMEM)],
        out_specs=(pl.BlockSpec(memory_space=pltpu.VMEM),) * 2,
        scratch_shapes=[pltpu.VMEM((2 * rows, width), jnp.bfloat16)] * 2,
        compiler_params=pltpu.CompilerParams(vmem_limit_bytes=48 * 2**20),
    )(embeddings)


def sum_in_pieces(packed, mean_rows):
    groups, wide = lax.axis_size("grp"), lax.axis_size("wide")
    core = lax.axis_index("wide") & 1
    twins = [(d, d ^ 1) for d in range(wide)]
    same_core = [list(range(c, wide, 2)) for c in range(2)]

    def over_grp(parts):
        return lax.all_to_all(parts, "grp", 0, 0)

    def over_wide(parts):
        return lax.all_to_all(parts, "wide", 0, 0, axis_index_groups=same_core)

    def spread(parts, trade, count):
        return trade(jnp.broadcast_to(parts[None], (count,) + parts.shape))

    half = packed.shape[0] // 2
    sent = lax.dynamic_slice_in_dim(packed, (1 - core) * half, half, 0)
    kept = lax.dynamic_slice_in_dim(packed, core * half, half, 0)
    piece = kept + lax.ppermute(sent, "wide", twins)
    piece = jnp.sum(over_grp(piece.reshape(groups, -1, LANES)), axis=0)
    piece = jnp.sum(over_wide(piece.reshape(wide // 2, -1, LANES)), axis=0)
    held = jnp.concatenate([piece, mean_rows], axis=0)
    held = spread(held, over_wide, wide // 2)
    held = spread(held, over_grp, groups)
    held = held.reshape((-1,) + held.shape[2:])
    other = lax.ppermute(held, "wide", twins)
    half = held.shape[0]
    return held, other, jnp.stack([core * half, (1 - core) * half])


def factor_block(block, upper_ref, inverse_ref):
    groups = LANES // SUB
    tiles = [block[SUB * p : SUB * (p + 1), :] for p in range(groups)]
    row_at = lax.broadcasted_iota(jnp.int32, (SUB, LANES), 0)
    lane_at = lax.broadcasted_iota(jnp.int32, (SUB, LANES), 1)
    unit = [
        jnp.where(lane_at == row_at + SUB * p, 1.0, 0.0).astype(jnp.float32)
        for p in range(groups)
    ]
    for g in range(groups):
        base = SUB * g
        ahead = g + 1 < groups
        rows = [over_rows(tiles[g], i) for i in range(SUB)]
        s = {
            (i, j): over_lanes(rows[i], base + j) for i in range(SUB) for j in range(i, SUB)
        }
        carried = [over_rows(unit[g], i) for i in range(SUB)]
        if ahead:
            column = [over_lanes(tiles[g + 1], base + i) for i in range(SUB)]
        scale = []
        for j in range(SUB):
            r = lax.rsqrt(s[j, j])
            scale.append(r)
            for k in range(j + 1, SUB):
                s[j, k] = s[j, k] * r
            for k in range(j + 1, SUB):
                for m in range(k, SUB):
                    s[k, m] = s[k, m] - s[j, k] * s[j, m]
            rows[j] = rows[j] * r
            carried[j] = carried[j] * r
            for k in range(j + 1, SUB):
                rows[k] = rows[k] - s[j, k] * rows[j]
                carried[k] = carried[k] - s[j, k] * carried[j]
            if ahead:
                column[j] = column[j] * r
                for k in range(j + 1, SUB):
                    column[k] = column[k] - column[j] * s[j, k]
                tiles[g + 1] = tiles[g + 1] - column[j] * rows[j]
                unit[g + 1] = unit[g + 1] - column[j] * carried[j]
            upper_ref[base + j : base + j + 1, :] = rows[j][:1, :]
            inverse_ref[base + j : base + j + 1, :] = carried[j][:1, :]
        if g + 2 < groups:
            for i in reversed(range(SUB)):
                for k in range(i + 1, SUB):
                    rows[i] = rows[i] - s[i, k] * rows[k]
                    carried[i] = carried[i] - s[i, k] * carried[k]
                rows[i] = rows[i] * scale[i]
                carried[i] = carried[i] * scale[i]
        for p in range(g + 2, groups):
            column = [over_lanes(tiles[p], base + i) for i in range(SUB)]
            tiles[p] = tiles[p] - tree_sum([c * x for c, x in zip(column, rows)])
            unit[p] = unit[p] - tree_sum([c * x for c, x in zip(column, carried)])
        yield


def tree_sum(terms):
    while len(terms) > 1:
        terms = [a + b for a, b in zip(terms[::2], terms[1::2])]
    return terms[0]


def in_three(values):
    high = values.astype(jnp.bfloat16)
    rest = values - high.astype(jnp.float32)
    middle = rest.astype(jnp.bfloat16)
    return high, middle, (rest - middle.astype(jnp.float32)).astype(jnp.bfloat16)


def left_parts(values):
    high, middle, low = in_three(values)
    return jnp.concatenate([high, middle], axis=1), jnp.concatenate([low, high], axis=1)


def right_parts(values):
    high, middle, low = in_three(values)
    stack = lambda a, b: jnp.concatenate([a, b], axis=0)
    return stack(high, high), stack(middle, middle), stack(high, low)


def parts_dot(left, right):
    plain = lambda a, b: fast_dot(a, b, ((1,), (0,)))
    return (plain(left[1], right[2]) + plain(left[0], right[1])) + plain(left[0], right[0])


def factor_kernel(
    held_ref,
    other_ref,
    numbers_ref,
    count_ref,
    factor_ref,
    high_ref,
    low_ref,
    mean_ref,
    work,
    packed,
    means_scr,
    upper_ref,
    inverse_ref,
):
    half = held_ref.shape[0]
    pieces = 2 * half
    width = factor_ref.shape[0]
    blocks = width // LANES
    piece_rows = packed.shape[0] // pieces

    for part, ref in enumerate((held_ref, other_ref)):

        def unpack(q, _):
            p = numbers_ref[part] ^ q
            to = pl.multiple_of(p * piece_rows, SUB)
            packed[pl.ds(to, piece_rows), :] = ref[q, :piece_rows, :]
            to = pl.multiple_of(p * SUB, SUB)
            means_scr[pl.ds(to, SUB), :] = ref[q, piece_rows : piece_rows + SUB, :]
            return 0

        lax.fori_loop(0, half, unpack, 0, unroll=True)

    stacked = means_scr[...].reshape(pieces, SUB, LANES)
    middle = jnp.mean(stacked, axis=0)
    apart = stacked - middle[None]
    wide = jnp.concatenate([apart[:, b, :] for b in range(blocks)], axis=1)
    for b in range(blocks):
        mean_ref[:, LANES * b : LANES * (b + 1)] = jnp.broadcast_to(
            middle[b : b + 1, :], (SUB, LANES)
        )
    total_scale = count_ref[1]
    place = {block: LANES * p for p, block in enumerate(upper_blocks(width))}
    span = lambda b, e=None: slice(LANES * b, LANES * (b + 1 if e is None else e))

    def gather(i, first, end):
        between = dot(wide[:, span(i)], wide[:, span(first, end)], ((0,), (0,)))
        for j in range(first, end):
            work[span(i), span(j)] = (
                packed[place[i, j] : place[i, j] + LANES, :]
                + between[:, span(j - first)] * count_ref[0]
            )

    def write_row(k):
        row_at = lax.broadcasted_iota(jnp.int32, (LANES, LANES), 0)
        col_at = lax.broadcasted_iota(jnp.int32, (LANES, LANES), 1)
        zero = jnp.zeros((LANES, LANES), jnp.float32)
        for j in range(blocks):
            if j < k:
                factor, back = zero, work[span(k), span(j)]
            elif j > k:
                factor, back = work[span(k), span(j)], zero
            else:
                factor = jnp.where(col_at >= row_at, upper_ref[k % 2], 0.0)
                back = inverse_ref[k % 2]
            factor_ref[span(k), span(j)] = factor * (1.0 / total_scale)
            high, low = split((back * total_scale).T)
            high_ref[span(j), span(k)] = high
            low_ref[span(j), span(k)] = low

    def below(k, i, left, right, first):
        change = parts_dot(left, [r[:, : LANES * (k + 1)] for r in right])
        if k:
            work[span(i), span(0, k)] = work[span(i), span(0, k)] - change[:, : LANES * k]
        work[span(i), span(k)] = -change[:, LANES * k :]
        if first < blocks:
            cols = span(first, blocks)
            work[span(i), cols] = work[span(i), cols] - parts_dot(
                left, [r[:, cols] for r in right]
            )

    def later(k, left, solved, turned):
        row = {}

        def solve_rest():
            if k:
                cols = span(0, k)
                work[span(k), cols] = parts_dot(left, right_parts(work[span(k), cols]))
            if k + 2 < blocks:
                cols = span(k + 2, blocks)
                work[span(k), cols] = parts_dot(left, right_parts(work[span(k), cols]))
            if k + 1 < blocks:
                work[span(k), span(k + 1)] = solved
            row["parts"] = right_parts(
                jnp.concatenate(
                    [
                        inverse_ref[k % 2] if j == k else work[span(k), span(j)]
                        for j in range(blocks)
                    ],
                    axis=1,
                )
            )

        todo = [solve_rest]
        for i in range(k + 1, blocks):

            def one(i=i):
                lead = turned if i == k + 1 else left_parts(work[span(k), span(i)].T)
                below(k, i, lead, row["parts"], max(i, k + 2))

            todo.append(one)
        todo.append(lambda: write_row(k))
        return todo

    gather(0, 0, 1)
    todo = [lambda: gather(0, 1, blocks)]
    todo += [lambda i=i: gather(i, i, blocks) for i in range(1, blocks)]
    for k in range(blocks):
        groups = LANES // SUB
        done = 0
        steps = factor_block(work[span(k), span(k)], upper_ref.at[k % 2], inverse_ref.at[k % 2])
        for g, _ in enumerate(steps):
            due = -(-len(todo) * (g + 1) // groups)
            for piece in todo[done:due]:
                piece()
            done = due
        left = left_parts(inverse_ref[k % 2])
        solved = turned = None
        if k + 1 < blocks:
            solved = parts_dot(left, right_parts(work[span(k), span(k + 1)]))
            turned = left_parts(solved.T)
            work[span(k + 1), span(k + 1)] = work[span(k + 1), span(k + 1)] - parts_dot(
                turned, right_parts(solved)
            )
        todo = later(k, left, solved, turned)
    for piece in todo:
        piece()


def factor_and_inverse(held, other, numbers, piece_rows, width, local_rows):
    pieces = 2 * held.shape[0]
    vmem = pl.BlockSpec(memory_space=pltpu.VMEM)
    smem = pl.BlockSpec(memory_space=pltpu.SMEM)
    half_type = jax.ShapeDtypeStruct((width, width), jnp.bfloat16)
    counts = jnp.array([local_rows, (local_rows * pieces) ** 0.5], jnp.float32)
    return pl.pallas_call(
        factor_kernel,
        out_shape=(
            jax.ShapeDtypeStruct((width, width), jnp.float32),
            half_type,
            half_type,
            jax.ShapeDtypeStruct((SUB, width), jnp.float32),
        ),
        in_specs=[vmem, vmem, smem, smem],
        out_specs=(vmem,) * 4,
        scratch_shapes=[
            pltpu.VMEM((width, width), jnp.float32),
            pltpu.VMEM((pieces * piece_rows, LANES), jnp.float32),
            pltpu.VMEM((pieces * SUB, LANES), jnp.float32),
            pltpu.VMEM((2, LANES, LANES), jnp.float32),
            pltpu.VMEM((2, LANES, LANES), jnp.float32),
        ],
        compiler_params=pltpu.CompilerParams(vmem_limit_bytes=48 * 2**20),
    )(held, other, numbers, counts)


def whiten_kernel(x_ref, mean_ref, high_ref, low_ref, out_ref):
    width = x_ref.shape[1]
    high, low = split(x_ref[...] - mean_ref[:1, :])
    for right in range(0, width, TILE):
        here = slice(right, right + TILE)
        deep = slice(0, right + TILE)
        tile = fast_dot(high[:, deep], high_ref[deep, here], ((1,), (0,)))
        tile = tile + fast_dot(high[:, deep], low_ref[deep, here], ((1,), (0,)))
        out_ref[:, here] = tile + fast_dot(low[:, deep], high_ref[deep, here], ((1,), (0,)))


def whiten(embeddings, mean, high, low):
    rows, width = embeddings.shape
    whole = lambda i: (0, 0)
    return pl.pallas_call(
        whiten_kernel,
        grid=(rows // TILE,),
        out_shape=jax.ShapeDtypeStruct((rows, width), jnp.float32),
        in_specs=[
            pl.BlockSpec((TILE, width), lambda i: (i, 0)),
            pl.BlockSpec(mean.shape, whole),
            pl.BlockSpec((width, width), whole),
            pl.BlockSpec((width, width), whole),
        ],
        out_specs=pl.BlockSpec((TILE, width), lambda i: (i, 0)),
        compiler_params=pltpu.CompilerParams(vmem_limit_bytes=48 * 2**20),
    )(embeddings, mean, high, low)


def shards(embeddings):
    local_rows, width = embeddings.shape
    devices = lax.axis_size("grp") * lax.axis_size("wide")
    used = LANES * len(upper_blocks(width))
    piece_rows = -(-used // (SUB * devices)) * SUB
    packed, mean_rows = local_gram(embeddings, piece_rows * devices, SUB)
    held, other, numbers = sum_in_pieces(packed, mean_rows)
    factor, high, low, mean = factor_and_inverse(
        held, other, numbers, piece_rows, width, local_rows
    )
    return (whiten(embeddings, mean, high, low), factor)


def solution(mesh):
    rows = P(AXES, None)
    return jax.shard_map(
        shards,
        mesh=mesh,
        in_specs=(rows,),
        out_specs=(rows, P()),
        check_vma=False,
    )
```
